32 devices in a mesh: chan: 8 (over z, y), row: 4 (over x, core).
Axes of the slice: x: 2, y: 2, z: 4, core: 2. Of those that a mesh axis runs over, the one named last changes fastest.
Arguments:
- voltages: bfloat16 [2, 2, 128, 256], P(None, None, None, 'chan'), may hold values from -6 to 6
- kernel_table: bfloat16 [4, 16, 16], replicated, may hold values from -6 to 6
- station_rows: int32 [256], replicated, may hold values from 0 to 752
- station_cols: int32 [256], replicated, may hold values from 0 to 752
- kernel_offset: int32 [256], replicated, may hold values from 0 to 3
Outputs:
- taylor_images: float32 [3, 768, 768], P(None, 'chan', 'row')
The draws below stay inside these ranges and needn't reach their ends.
Inputs may be any that keep to these rules, and one draw needn't show every extreme that they name: `station_rows`: kernels lie inside the grid. `station_cols`: kernels lie inside the grid.
All inputs are finite; a program needn't handle non-finite values.
Results may differ from the reference program's by a relative error of at most 0.0013.
Values may be sent and summed in bfloat16 or wider, within the bound.
No kernel may reach another device: no remote copies, remote signals or barrier semaphores. Data moves between devices by JAX's collectives and lax.ppermute only.
A program may use at most 128 MiB of HBM per device.

```python
import jax
import jax.numpy as jnp
from jax import lax

S = 256
F = 128
G = 768
K = 16
NOFF = 4
TT = 2


def with_ends(values, stream_key, least, high):
    extent = values.shape
    place = [jax.random.randint(jax.random.fold_in(stream_key, axis), (), 0, extent[axis]) for axis in range(len(extent))]
    values = values.at[tuple(place)].set(least)
    longest = extent.index(max(extent))
    place[longest] = (place[longest] + 1) % extent[longest]
    return values.at[tuple(place)].set(high)


def block_scale(stream_key, extent, cuts, least, top_value):
    def one(dim, parts):
        steps = jax.random.uniform(jax.random.fold_in(jax.random.fold_in(stream_key, 6), dim), (parts,), jnp.float32, least / len(cuts), top_value / len(cuts))
        return jnp.repeat(jnp.exp(steps), extent[dim] // parts).reshape((-1,) + (1,) * (len(extent) - dim - 1))

    loudness = one(*cuts[0])
    for cut in cuts[1:]:
        loudness = loudness * one(*cut)
    return loudness


def bell_draw(rng, dims, deviation, bound, pieces=(), kind=jnp.bfloat16):
    array = jax.random.normal(rng, dims, jnp.float32) * deviation
    if len(pieces) > 0:
        array = block_scale(rng, dims, pieces, -0.22, 0.18) * array
    return jnp.clip(array, min=-bound, max=bound).astype(kind)


def setup_inputs(seed: int = 0) -> dict:
    arg_keys = jax.random.split(jax.random.key(seed), 6)
    return {
        "voltages": bell_draw(arg_keys[0], (2, TT, F, S), 1.0, 6.0, ((3, 8),)),
        "kernel_table": bell_draw(arg_keys[1], (NOFF, K, K), 1.0, 6.0),
        "station_rows": with_ends(jax.random.randint(arg_keys[2], (S,), 0, G - K + 1), jax.random.fold_in(arg_keys[2], 1), 0, G - K).astype(jnp.int32),
        "station_cols": with_ends(jax.random.randint(arg_keys[3], (S,), 0, G - K + 1), jax.random.fold_in(arg_keys[3], 1), 0, G - K).astype(jnp.int32),
        "kernel_offset": with_ends(jax.random.randint(arg_keys[4], (S,), 0, NOFF), jax.random.fold_in(arg_keys[4], 1), 0, NOFF - 1).astype(jnp.int32),
    }


def twiddles(length):
    index = jnp.arange(length, dtype=jnp.int32)
    product = index[:, None] * index[None, :] % length
    angle = 2.0 * jnp.pi / length * product.astype(jnp.float32)
    return (jnp.cos(angle).astype(jnp.bfloat16), jnp.sin(angle).astype(jnp.bfloat16))

def taylor_weights(count):
    chans = jnp.arange(count, dtype=jnp.int32).astype(jnp.float32)
    coord = (2.0 * chans + 1.0 - count) / count
    stacked = jnp.stack([jnp.ones_like(coord), coord, coord * coord])
    return stacked / jnp.sqrt(lax.optimization_barrier(jnp.sum(stacked * stacked, axis=1, keepdims=True)))

def reference(voltages, kernel_table, station_rows, station_cols, kernel_offset):
    cosine_table, sine_table = twiddles(G)
    cos_wide = cosine_table.astype(jnp.float32)
    sin_wide = sine_table.astype(jnp.float32)
    kernels = kernel_table[kernel_offset].astype(jnp.float32)
    offsets = jnp.arange(K, dtype=jnp.int32)
    zero_grid = jnp.zeros((K, K), jnp.int32)
    rows_index = station_rows[:, None, None] + offsets[None, :, None] + zero_grid[None]
    cols_index = station_cols[:, None, None] + offsets[None, None, :] + zero_grid[None]
    weights = taylor_weights(F)
    scale = 1.0 / (TT * S * K * K)
    high = lax.Precision.HIGHEST

    def per_channel(summed, channel):
        volt = lax.dynamic_index_in_dim(voltages, channel, 2, keepdims=False).astype(jnp.float32)
        values = volt[:, :, :, None, None] * kernels[None, None]
        grid = jnp.zeros((2, TT, G, G), jnp.float32).at[:, :, rows_index, cols_index].add(values)
        aperture = lax.optimization_barrier(grid.astype(jnp.bfloat16)).astype(jnp.float32)
        real_grid, imag_grid = (aperture[0], aperture[1])
        real_half = jnp.matmul(real_grid, cos_wide, precision=high) + jnp.matmul(imag_grid, sin_wide, precision=high)
        imag_half = jnp.matmul(imag_grid, cos_wide, precision=high) - jnp.matmul(real_grid, sin_wide, precision=high)
        real_half = lax.optimization_barrier(real_half.astype(jnp.bfloat16)).astype(jnp.float32)
        imag_half = lax.optimization_barrier(imag_half.astype(jnp.bfloat16)).astype(jnp.float32)
        real_field = jnp.einsum('ru,trk->tuk', cos_wide, real_half, precision=high) + jnp.einsum('ru,trk->tuk', sin_wide, imag_half, precision=high)
        imag_field = jnp.einsum('ru,trk->tuk', cos_wide, imag_half, precision=high) - jnp.einsum('ru,trk->tuk', sin_wide, real_half, precision=high)
        intensity = lax.optimization_barrier(jnp.sum(real_field * real_field + imag_field * imag_field, axis=0)) * scale
        column = lax.dynamic_index_in_dim(weights, channel, 1, keepdims=False)
        return (summed + column[:, None, None] * intensity[None], None)
    start = jnp.zeros((3, G, G), jnp.float32)
    taylor_images, _ = lax.scan(per_channel, start, jnp.arange(F, dtype=jnp.int32))
    return taylor_images
```

```python
import jax
import jax.numpy as jnp
import numpy as np
from jax import lax
from jax.experimental import pallas as pl
from jax.experimental.pallas import tpu as pltpu
from jax.sharding import PartitionSpec as P

TILE = 256
STEP = 4


def wave_fit(terms=8):
    nodes = 0.125 + 0.125 * np.cos(np.pi * (np.arange(200) + 0.5) / 200)
    root = np.sqrt(nodes)
    fit = np.polynomial.polynomial.polyfit
    cosine = fit(nodes, np.cos(2 * np.pi * root), terms - 1)
    sine = fit(nodes, np.sin(2 * np.pi * root) / root, terms - 1)
    return [float(c) for c in cosine], [float(c) for c in sine]


COS_FIT, SIN_FIT = wave_fit()


def horner(coefs, x):
    value = jnp.full_like(x, coefs[-1])
    for c in coefs[-2::-1]:
        value = value * x + c
    return value


def wave(product, cells):
    turns = product * (1.0 / cells)
    part = (product - cells * jnp.round(turns)) * (1.0 / cells)
    square = part * part
    return horner(COS_FIT, square), -part * horner(SIN_FIT, square)


def image_kernel(
    cells, width, volts, rows, cols, variant, first_col, phase_re, phase_im, spread_re, spread_im,
    coord, out, volt_re, volt_im, base_re, base_im, pick, x_a, x_b, h_a, h_b,
):
    stations = rows.shape[0]
    planes = volts.shape[0] // 2
    lanes = STEP * width
    steps = phase_re.shape[0]
    chans = coord.shape[0]
    volt_re[...] = volts[:planes, :].astype(jnp.float32)
    volt_im[...] = volts[planes:, :].astype(jnp.float32)
    pick[...] = jnp.broadcast_to(variant[...], (stations, 128))
    row_of = jnp.broadcast_to(rows[...].astype(jnp.float32), (stations, 128))
    col_of = jnp.broadcast_to(cols[...].astype(jnp.float32), (stations, 128))
    first = first_col[0].astype(jnp.float32)
    for tile in range(lanes // 128):
        place = lax.broadcasted_iota(jnp.int32, (stations, 128), 1) + tile * 128
        down = jnp.zeros((stations, 128), jnp.float32)
        for p in range(1, STEP):
            down = jnp.where(place >= p * width, float(p), down)
        across = place.astype(jnp.float32) - down * width + first
        real, imag = wave(row_of * down + col_of * across, cells)
        base_re[:, tile * 128:(tile + 1) * 128] = real
        base_im[:, tile * 128:(tile + 1) * 128] = imag

    def prepare(q, x_out, h_out):
        pr = phase_re[pl.ds(q, 1), :]
        pi = phase_im[pl.ds(q, 1), :]
        vr = volt_re[...]
        vi = volt_im[...]
        xr = (vr * pr - vi * pi).astype(jnp.bfloat16)
        xi = (vr * pi + vi * pr).astype(jnp.bfloat16)
        x_out[:planes, :stations] = xr
        x_out[:planes, stations:] = -xi
        x_out[planes:, :stations] = xi
        x_out[planes:, stations:] = xr
        for tile in range(lanes // 128):
            at = slice(tile * 128, (tile + 1) * 128)
            gr = spread_re[q, :, at]
            gi = spread_im[q, :, at]
            for group in range(stations // 16):
                parts_re = []
                parts_im = []
                for half in range(2):
                    sub = slice(group * 16 + half * 8, group * 16 + half * 8 + 8)
                    index = pick[sub, :]
                    sr = jnp.take_along_axis(gr, index, axis=0)
                    si = jnp.take_along_axis(gi, index, axis=0)
                    br = base_re[sub, at]
                    bi = base_im[sub, at]
                    parts_re.append(br * sr - bi * si)
                    parts_im.append(br * si + bi * sr)
                pair = slice(group * 16, group * 16 + 16)
                low = slice(stations + group * 16, stations + group * 16 + 16)
                h_out[pair, at] = jnp.concatenate(parts_re, axis=0).astype(jnp.bfloat16)
                h_out[low, at] = jnp.concatenate(parts_im, axis=0).astype(jnp.bfloat16)

    def finish(q, x_in, h_in):
        for tile in range(lanes // TILE):
            at = slice(tile * TILE, (tile + 1) * TILE)
            field = jnp.dot(x_in[...], h_in[:, at], preferred_element_type=jnp.float32)
            power = field * field
            total = power[:planes] + power[planes:]
            total = total[:chans] + total[chans:]
            x = jnp.concatenate([coord[...]] * (TILE // 128), axis=1)
            first_order = total * x
            second_order = first_order * x
            for k, value in enumerate((total, first_order, second_order)):
                out[q, k:k + 1, at] = jnp.sum(value, axis=0, keepdims=True)

    prepare(0, x_a, h_a)

    def two(i, carry):
        prepare(2 * i + 1, x_b, h_b)
        finish(2 * i, x_a, h_a)
        prepare(jnp.minimum(2 * i + 2, steps - 1), x_a, h_a)
        finish(2 * i + 1, x_b, h_b)
        return carry

    lax.fori_loop(0, steps // 2, two, 0)


def angle_of(product, cells):
    return (product % cells).astype(jnp.float32) * (2.0 * np.pi / cells)


def local(cells, voltages, kernel_table, station_rows, station_cols, kernel_offset):
    high = lax.Precision.HIGHEST
    times, chans = voltages.shape[1], voltages.shape[2]
    stations = station_rows.shape[0]
    variants, width_k = kernel_table.shape[0], kernel_table.shape[1]
    height = cells // lax.axis_size("chan")
    width = cells // lax.axis_size("row")
    first_row = lax.axis_index("chan") * height
    first_col = lax.axis_index("row") * width
    steps = height // STEP
    lanes = STEP * width

    planes = times * chans
    gathered = lax.all_gather(voltages.reshape(2 * planes, voltages.shape[3]), "chan", axis=1, tiled=True)

    start = first_row + STEP * jnp.arange(steps, dtype=jnp.int32)
    turn = angle_of(start[:, None] * station_rows[None, :], cells)
    phase_re, phase_im = jnp.cos(turn), -jnp.sin(turn)

    taps = jnp.arange(width_k, dtype=jnp.int32)
    turn_u = angle_of((first_row + jnp.arange(height, dtype=jnp.int32))[:, None] * taps[None, :], cells)
    turn_v = angle_of((first_col + jnp.arange(width, dtype=jnp.int32))[:, None] * taps[None, :], cells)
    table = kernel_table.astype(jnp.float32)
    half_re = jnp.einsum("oab,vb->oav", table, jnp.cos(turn_v), precision=high)
    half_im = -jnp.einsum("oab,vb->oav", table, jnp.sin(turn_v), precision=high)
    cu, su = jnp.cos(turn_u), jnp.sin(turn_u)
    spread_re = jnp.einsum("ua,oav->uov", cu, half_re, precision=high) + jnp.einsum(
        "ua,oav->uov", su, half_im, precision=high
    )
    spread_im = jnp.einsum("ua,oav->uov", cu, half_im, precision=high) - jnp.einsum(
        "ua,oav->uov", su, half_re, precision=high
    )

    def pack(s):
        s = s.reshape(steps, STEP, variants, width).transpose(0, 2, 1, 3).reshape(steps, variants, lanes)
        return jnp.pad(s, ((0, 0), (0, 8 - variants), (0, 0)))

    x = (2.0 * np.arange(chans) + 1.0 - chans) / chans
    coord = jnp.asarray(np.broadcast_to(x[:, None], (chans, 128)), jnp.float32)
    vmem = pl.BlockSpec(memory_space=pltpu.VMEM)
    smem = pl.BlockSpec(memory_space=pltpu.SMEM)
    raw = pl.pallas_call(
        lambda *refs: image_kernel(cells, width, *refs),
        out_shape=jax.ShapeDtypeStruct((steps, 3, lanes), jnp.float32),
        in_specs=[vmem, vmem, vmem, vmem, smem, vmem, vmem, vmem, vmem, vmem],
        out_specs=vmem,
        scratch_shapes=[
            pltpu.VMEM((planes, stations), jnp.float32),
            pltpu.VMEM((planes, stations), jnp.float32),
            pltpu.VMEM((stations, lanes), jnp.float32),
            pltpu.VMEM((stations, lanes), jnp.float32),
            pltpu.VMEM((stations, 128), jnp.int32),
            pltpu.VMEM((2 * planes, 2 * stations), jnp.bfloat16),
            pltpu.VMEM((2 * planes, 2 * stations), jnp.bfloat16),
            pltpu.VMEM((2 * stations, lanes), jnp.bfloat16),
            pltpu.VMEM((2 * stations, lanes), jnp.bfloat16),
        ],
        compiler_params=pltpu.CompilerParams(vmem_limit_bytes=40 * 1024 * 1024),
    )(
        gathered, station_rows[:, None], station_cols[:, None], kernel_offset[:, None],
        first_col.reshape(1).astype(jnp.int32), phase_re, phase_im, pack(spread_re), pack(spread_im), coord,
    )
    norm = np.array([1.0 / np.sqrt(np.sum(x ** (2 * k))) for k in range(3)]) / (times * stations * width_k * width_k)
    images = raw.reshape(steps, 3, STEP, width).transpose(1, 0, 2, 3).reshape(3, height, width)
    return images * jnp.asarray(norm, jnp.float32)[:, None, None]


def solution(mesh):
    cells = 768
    placed = (P(None, None, None, "chan"), P(), P(), P(), P())
    return jax.shard_map(
        lambda *args: local(cells, *args), mesh=mesh, in_specs=placed, out_specs=P(None, "chan", "row"), check_vma=False
    )
```

```python
import jax
import jax.numpy as jnp
import numpy as np
from jax import lax
from jax.experimental import pallas as pl
from jax.experimental.pallas import tpu as pltpu
from jax.sharding import PartitionSpec as P

TILE = 256
STEP = 4


def wave_fit(terms=8):
    nodes = 0.125 + 0.125 * np.cos(np.pi * (np.arange(200) + 0.5) / 200)
    root = np.sqrt(nodes)
    fit = np.polynomial.polynomial.polyfit
    cosine = fit(nodes, np.cos(2 * np.pi * root), terms - 1)
    sine = fit(nodes, np.sin(2 * np.pi * root) / root, terms - 1)
    return [float(c) for c in cosine], [float(c) for c in sine]


COS_FIT, SIN_FIT = wave_fit()


def horner(coefs, x):
    value = jnp.full_like(x, coefs[-1])
    for c in coefs[-2::-1]:
        value = value * x + c
    return value


def wave(product, cells):
    turns = product * (1.0 / cells)
    part = (product - cells * jnp.round(turns)) * (1.0 / cells)
    square = part * part
    return horner(COS_FIT, square), -part * horner(SIN_FIT, square)


def response_kernel(
    cells, width, rows, cols, variant, first_col, spread_re, spread_im, response, base_re, base_im, pick
):
    stations = rows.shape[0]
    lanes = STEP * width

    @pl.when(pl.program_id(0) == 0)
    def _():
        pick[...] = jnp.broadcast_to(variant[...], (stations, 128))
        row_of = jnp.broadcast_to(rows[...].astype(jnp.float32), (stations, 128))
        col_of = jnp.broadcast_to(cols[...].astype(jnp.float32), (stations, 128))
        first = first_col[0].astype(jnp.float32)
        for tile in range(lanes // 128):
            place = lax.broadcasted_iota(jnp.int32, (stations, 128), 1) + tile * 128
            down = jnp.zeros((stations, 128), jnp.float32)
            for p in range(1, STEP):
                down = jnp.where(place >= p * width, float(p), down)
            across = place.astype(jnp.float32) - down * width + first
            real, imag = wave(row_of * down + col_of * across, cells)
            base_re[:, tile * 128:(tile + 1) * 128] = real
            base_im[:, tile * 128:(tile + 1) * 128] = imag

    for tile in range(lanes // 128):
        at = slice(tile * 128, (tile + 1) * 128)
        gr = spread_re[0, :, at]
        gi = spread_im[0, :, at]
        for group in range(stations // 16):
            parts_re = []
            parts_im = []
            for half in range(2):
                sub = slice(group * 16 + half * 8, group * 16 + half * 8 + 8)
                index = pick[sub, :]
                sr = jnp.take_along_axis(gr, index, axis=0)
                si = jnp.take_along_axis(gi, index, axis=0)
                br = base_re[sub, at]
                bi = base_im[sub, at]
                parts_re.append(br * sr - bi * si)
                parts_im.append(br * si + bi * sr)
            pair = slice(group * 16, group * 16 + 16)
            low = slice(stations + group * 16, stations + group * 16 + 16)
            response[0, pair, at] = jnp.concatenate(parts_re, axis=0).astype(jnp.bfloat16)
            response[0, low, at] = jnp.concatenate(parts_im, axis=0).astype(jnp.bfloat16)


def image_kernel(chans, pieces, phase_re, phase_im, coord, response, out, volt_re, volt_im, x_a, x_b):
    planes, stations = volt_re.shape
    lanes = response.shape[2]
    steps = phase_re.shape[0]
    step = pl.program_id(0)

    def prepare(q, x_out):
        pr = phase_re[pl.ds(q, 1), :]
        pi = phase_im[pl.ds(q, 1), :]
        vr = volt_re[...]
        vi = volt_im[...]
        xr = (vr * pr - vi * pi).astype(jnp.bfloat16)
        xi = (vr * pi + vi * pr).astype(jnp.bfloat16)
        x_out[:planes, :stations] = xr
        x_out[:planes, stations:] = -xi
        x_out[planes:, :stations] = xi
        x_out[planes:, stations:] = xr

    def finish(part, x_in):
        for tile in range(lanes // TILE):
            at = slice(tile * TILE, (tile + 1) * TILE)
            field = jnp.dot(x_in[...], response[part, :, at], preferred_element_type=jnp.float32)
            power = field * field
            total = power[:planes] + power[planes:]
            total = total[:chans] + total[chans:]
            x = jnp.concatenate([coord[...]] * (TILE // 128), axis=1)
            first_order = total * x
            second_order = first_order * x
            for k, value in enumerate((total, first_order, second_order)):
                out[part, k:k + 1, at] = jnp.sum(value, axis=0, keepdims=True)

    @pl.when(step == 0)
    def _():
        blocks = [piece[...].astype(jnp.float32) for piece in pieces]
        count = blocks[0].shape[0] // (2 * planes // chans)
        for plane in range(2 * planes // chans):
            turned = jnp.concatenate([b[plane * count:(plane + 1) * count] for b in blocks], axis=0).T
            target = volt_re if plane < planes // chans else volt_im
            at = plane % (planes // chans) * chans
            target[at:at + chans, :] = turned
        prepare(0, x_a)

    prepare(2 * step + 1, x_b)
    finish(0, x_a)
    prepare(jnp.minimum(2 * step + 2, steps - 1), x_a)
    finish(1, x_b)


def angle_of(product, cells):
    return (product % cells).astype(jnp.float32) * (2.0 * np.pi / cells)


def local(cells, voltages, kernel_table, station_rows, station_cols, kernel_offset):
    high = lax.Precision.HIGHEST
    times, chans = voltages.shape[1], voltages.shape[2]
    stations = station_rows.shape[0]
    variants, width_k = kernel_table.shape[0], kernel_table.shape[1]
    height = cells // lax.axis_size("chan")
    width = cells // lax.axis_size("row")
    first_row = lax.axis_index("chan") * height
    first_col = lax.axis_index("row") * width
    steps = height // STEP
    lanes = STEP * width

    planes = times * chans
    count = lax.axis_size("chan")
    here = lax.axis_index("chan")
    own = voltages.transpose(0, 1, 3, 2).reshape(2 * times * voltages.shape[3], chans)
    pieces = [own] + [
        lax.ppermute(own, "chan", [(j, (j + k) % count) for j in range(count)]) for k in range(1, count)
    ]

    def arrival_order(values):
        turned = values.reshape(count, stations // count)[::-1]
        return lax.dynamic_slice_in_dim(jnp.concatenate([turned, turned]), count - 1 - here, count, 0).reshape(-1)

    station_rows = arrival_order(station_rows)
    station_cols = arrival_order(station_cols)
    kernel_offset = arrival_order(kernel_offset)

    start = first_row + STEP * jnp.arange(steps, dtype=jnp.int32)
    turn = angle_of(start[:, None] * station_rows[None, :], cells)
    phase_re, phase_im = jnp.cos(turn), -jnp.sin(turn)

    taps = jnp.arange(width_k, dtype=jnp.int32)
    turn_u = angle_of((first_row + jnp.arange(height, dtype=jnp.int32))[:, None] * taps[None, :], cells)
    turn_v = angle_of((first_col + jnp.arange(width, dtype=jnp.int32))[:, None] * taps[None, :], cells)
    table = kernel_table.astype(jnp.float32)
    half_re = jnp.einsum("oab,vb->oav", table, jnp.cos(turn_v), precision=high)
    half_im = -jnp.einsum("oab,vb->oav", table, jnp.sin(turn_v), precision=high)
    cu, su = jnp.cos(turn_u), jnp.sin(turn_u)
    spread_re = jnp.einsum("ua,oav->uov", cu, half_re, precision=high) + jnp.einsum(
        "ua,oav->uov", su, half_im, precision=high
    )
    spread_im = jnp.einsum("ua,oav->uov", cu, half_im, precision=high) - jnp.einsum(
        "ua,oav->uov", su, half_re, precision=high
    )

    def pack(s):
        s = s.reshape(steps, STEP, variants, width).transpose(0, 2, 1, 3).reshape(steps, variants, lanes)
        return jnp.pad(s, ((0, 0), (0, 8 - variants), (0, 0)))

    x = (2.0 * np.arange(chans) + 1.0 - chans) / chans
    coord = jnp.asarray(np.broadcast_to(x[:, None], (chans, 128)), jnp.float32)
    vmem = pl.BlockSpec(memory_space=pltpu.VMEM)
    smem = pl.BlockSpec(memory_space=pltpu.SMEM)
    spread = pl.BlockSpec((1, 8, lanes), lambda i: (i, 0, 0))
    response = pl.pallas_call(
        lambda *refs: response_kernel(cells, width, *refs),
        grid=(steps,),
        out_shape=jax.ShapeDtypeStruct((steps, 2 * stations, lanes), jnp.bfloat16),
        in_specs=[vmem, vmem, vmem, smem, spread, spread],
        out_specs=pl.BlockSpec((1, 2 * stations, lanes), lambda i: (i, 0, 0)),
        scratch_shapes=[
            pltpu.VMEM((stations, lanes), jnp.float32),
            pltpu.VMEM((stations, lanes), jnp.float32),
            pltpu.VMEM((stations, 128), jnp.int32),
        ],
        compiler_params=pltpu.CompilerParams(vmem_limit_bytes=16 * 1024 * 1024),
        cost_estimate=pl.CostEstimate(
            flops=16 * steps * stations * lanes, bytes_accessed=4 * steps * stations * lanes, transcendentals=0
        ),
    )(
        station_rows[:, None], station_cols[:, None], kernel_offset[:, None],
        first_col.reshape(1).astype(jnp.int32), pack(spread_re), pack(spread_im),
    )
    raw = pl.pallas_call(
        lambda *refs: image_kernel(chans, refs[:count], *refs[count:]),
        grid=(steps // 2,),
        out_shape=jax.ShapeDtypeStruct((steps, 3, lanes), jnp.float32),
        in_specs=[vmem] * (count + 3) + [pl.BlockSpec((2, 2 * stations, lanes), lambda i: (i, 0, 0))],
        out_specs=pl.BlockSpec((2, 3, lanes), lambda i: (i, 0, 0)),
        scratch_shapes=[
            pltpu.VMEM((planes, stations), jnp.float32),
            pltpu.VMEM((planes, stations), jnp.float32),
            pltpu.VMEM((2 * planes, 2 * stations), jnp.bfloat16),
            pltpu.VMEM((2 * planes, 2 * stations), jnp.bfloat16),
        ],
        compiler_params=pltpu.CompilerParams(vmem_limit_bytes=24 * 1024 * 1024),
        cost_estimate=pl.CostEstimate(
            flops=8 * steps * planes * stations * lanes, bytes_accessed=4 * steps * stations * lanes, transcendentals=0
        ),
    )(*pieces, phase_re, phase_im, coord, response)
    norm = np.array([1.0 / np.sqrt(np.sum(x ** (2 * k))) for k in range(3)]) / (times * stations * width_k * width_k)
    images = raw.reshape(steps, 3, STEP, width).transpose(1, 0, 2, 3).reshape(3, height, width)
    return images * jnp.asarray(norm, jnp.float32)[:, None, None]


def solution(mesh):
    cells = 768
    placed = (P(None, None, None, "chan"), P(), P(), P(), P())
    return jax.shard_map(
        lambda *args: local(cells, *args), mesh=mesh, in_specs=placed, out_specs=P(None, "chan", "row"), check_vma=False
    )
```

```python
import jax
import jax.numpy as jnp
import numpy as np
from jax import lax
from jax.experimental import pallas as pl
from jax.experimental.pallas import tpu as pltpu
from jax.sharding import PartitionSpec as P

TILE = 256
STEP = 4


def wave_fit(terms=8):
    nodes = 0.125 + 0.125 * np.cos(np.pi * (np.arange(200) + 0.5) / 200)
    root = np.sqrt(nodes)
    fit = np.polynomial.polynomial.polyfit
    cosine = fit(nodes, np.cos(2 * np.pi * root), terms - 1)
    sine = fit(nodes, np.sin(2 * np.pi * root) / root, terms - 1)
    return [float(c) for c in cosine], [float(c) for c in sine]


COS_FIT, SIN_FIT = wave_fit()


def horner(coefs, x):
    value = jnp.full_like(x, coefs[-1])
    for c in coefs[-2::-1]:
        value = value * x + c
    return value


def wave(product, cells):
    turns = product * (1.0 / cells)
    part = (product - cells * jnp.round(turns)) * (1.0 / cells)
    square = part * part
    return horner(COS_FIT, square), -part * horner(SIN_FIT, square)


def whole_of(shape, axis):
    return lax.broadcasted_iota(jnp.int32, shape, axis)


def split(value):
    high = value.astype(jnp.bfloat16)
    return high, (value - high.astype(jnp.float32)).astype(jnp.bfloat16)


def station_column(values, stations):
    return jnp.broadcast_to(values.astype(jnp.float32), (128, stations)).T


def table_kernel(
    cells, width, held, place, rows, cols, variant, table, base_re, base_im, pick, spread_re, spread_im, kept
):
    kept[...] = held[...]
    stations = rows.shape[1]
    steps, lanes = spread_re.shape[0], spread_re.shape[2]
    taps = table.shape[1]
    variants = table.shape[0] // taps
    first_row = place[1].astype(jnp.float32)
    first_col = place[2].astype(jnp.float32)
    pick[...] = station_column(variant[...], stations).astype(jnp.int32)
    row_of = station_column(rows[...], stations)
    col_of = station_column(cols[...], stations)

    def down_across(shape, start):
        lane = whole_of(shape, 1) + start
        down = jnp.zeros(shape, jnp.float32)
        for p in range(1, STEP):
            down = jnp.where(lane >= p * width, float(p), down)
        return down, lane.astype(jnp.float32) - down * width + first_col

    for tile in range(lanes // 128):
        at = slice(tile * 128, (tile + 1) * 128)
        down, across = down_across((stations, 128), tile * 128)
        base_re[:, at], base_im[:, at] = wave(row_of * down + col_of * across, cells)

    down, across = down_across((taps, lanes), 0)
    tap = whole_of((taps, lanes), 0).astype(jnp.float32)
    kernels = table[...]

    def over_columns(value):
        high, low = split(value)
        return jnp.dot(kernels, high, preferred_element_type=jnp.float32) + jnp.dot(
            kernels, low, preferred_element_type=jnp.float32
        )

    half_re, half_im = [over_columns(value) for value in wave(tap * across, cells)]
    turn_re, turn_im = wave(tap * down, cells)
    tall = -(-steps // 16) * 16
    lane = whole_of((tall, 6 * taps), 1)
    start = first_row + float(STEP) * whole_of((tall, 6 * taps), 0).astype(jnp.float32)
    left_re, left_im = wave(start * (lane % taps).astype(jnp.float32), cells)
    value = jnp.where(lane // taps % 2 == 0, left_re, -left_im)
    high, low = split(value)
    left = jnp.where(lane // (2 * taps) == 1, low.astype(jnp.float32), high.astype(jnp.float32)).astype(jnp.bfloat16)
    for o in range(variants):
        rows_o = slice(o * taps, (o + 1) * taps)
        real = turn_re * half_re[rows_o] - turn_im * half_im[rows_o]
        imag = turn_re * half_im[rows_o] + turn_im * half_re[rows_o]
        for target, one, two in ((spread_re, real, imag), (spread_im, imag, -real)):
            one_high, one_low = split(one)
            two_high, two_low = split(two)
            right = jnp.concatenate([one_high, two_high, one_high, two_high, one_low, two_low], axis=0)
            target[:, o, :] = jnp.dot(left, right, preferred_element_type=jnp.float32)[:steps]


def response_kernel(first, held, base_re, base_im, pick, spread_re, spread_im, response, kept):
    kept[...] = held[...]
    parts, stations, lanes = response.shape[0], base_re.shape[0], base_re.shape[1]

    def two(i, carry):
        for tile in range(lanes // 128):
            at = slice(tile * 128, (tile + 1) * 128)
            tables = [(spread_re[first + 2 * i + j, :, at], spread_im[first + 2 * i + j, :, at]) for j in range(2)]
            for group in range(stations // 16):
                made = [([], []), ([], [])]
                for half in range(2):
                    sub = slice(group * 16 + half * 8, group * 16 + half * 8 + 8)
                    index = pick[sub, :]
                    br = base_re[sub, at]
                    bi = base_im[sub, at]
                    for j in range(2):
                        sr = jnp.take_along_axis(tables[j][0], index, axis=0)
                        si = jnp.take_along_axis(tables[j][1], index, axis=0)
                        made[j][0].append(br * sr - bi * si)
                        made[j][1].append(br * si + bi * sr)
                pair = slice(group * 16, group * 16 + 16)
                low = slice(stations + group * 16, stations + group * 16 + 16)
                for j in range(2):
                    response[2 * i + j, pair, at] = jnp.concatenate(made[j][0], axis=0).astype(jnp.bfloat16)
                    response[2 * i + j, low, at] = jnp.concatenate(made[j][1], axis=0).astype(jnp.bfloat16)
        return carry

    lax.fori_loop(0, parts // 2, two, 0)


def image_kernel(
    cells, chans, width, norm, masks, groups, place, rows, *refs
):
    blocks, responses = refs[:groups[0]], refs[groups[0]:sum(groups)]
    out, turned, volt_re, volt_im, phase_re, phase_im, x_a, x_b, f_a, f_b, sums, strips = refs[sum(groups):]
    planes, stations = volt_re.shape
    steps, lanes = phase_re.shape[0], responses[0].shape[2]
    sheets = turned.shape[0]
    each = stations // len(sum(masks, ()))

    for block, held in zip(blocks, masks):
        value = block[...].astype(jnp.float32)
        for n, mask in enumerate(held):
            at = pl.multiple_of((place[0] ^ mask) * each, 8)
            for sheet in range(sheets):
                line = (n * sheets + sheet) * each
                turned[sheet, pl.ds(at, each), :] = value[line:line + each]
    for sheet in range(sheets):
        target = volt_re if sheet < sheets // 2 else volt_im
        at = sheet % (sheets // 2) * chans
        target[at:at + chans, :] = turned[sheet].T
    start = place[1].astype(jnp.float32) + float(STEP) * whole_of((steps, stations), 0).astype(jnp.float32)
    phase_re[...], phase_im[...] = wave(start * rows[...].astype(jnp.float32), cells)

    def prepare(q, x_out):
        pr = phase_re[pl.ds(q, 1), :]
        pi = phase_im[pl.ds(q, 1), :]
        vr = volt_re[...]
        vi = volt_im[...]
        xr = (vr * pr - vi * pi).astype(jnp.bfloat16)
        xi = (vr * pi + vi * pr).astype(jnp.bfloat16)
        x_out[:planes, :stations] = xr
        x_out[:planes, stations:] = -xi
        x_out[planes:, :stations] = xi
        x_out[planes:, stations:] = xr

    step_of = (2.0 * whole_of((8, TILE), 0).astype(jnp.float32) + 1.0 - chans) * 0.0625

    def collect(q, tile, field):
        zero = jnp.zeros((8, TILE), jnp.float32)
        s0, s1, s2 = zero, zero, zero
        for g in range(chans // 8 - 1, -1, -1):
            for t in range(2 * planes // chans):
                line = t * chans + g * 8
                part = field[line:line + 8, :]
                total = part * part if t == 0 else total + part * part
            s0 = s0 + total
            s1 = s1 + s0
            s2 = s2 + s1
        g1 = s1 - s0
        g2 = 2.0 * s2 - 3.0 * s1 + s0
        first = g1 + step_of * s0
        second = g2 + step_of * (2.0 * g1 + step_of * s0)
        for k, value in enumerate((s0, first, second)):
            sums[k, pl.ds(q, 1), tile * TILE:(tile + 1) * TILE] = norm[k] * jnp.sum(value, axis=0, keepdims=True)

    tiles = lanes // TILE
    fields = (f_a, f_b)
    prepare(0, x_a)
    f_b[...] = jnp.zeros_like(f_b)
    for part, response in enumerate(responses):
        base = part * response.shape[0]

        def two(i, carry):
            q = base + 2 * i
            for n in range(2 * tiles):
                x = x_a if n < tiles else x_b
                at = slice(n % tiles * TILE, (n % tiles + 1) * TILE)
                fields[n % 2][...] = jnp.dot(
                    x[...], response[2 * i + n // tiles, :, at], preferred_element_type=jnp.float32
                )
                if n == 0:
                    collect(jnp.maximum(q - 1, 0), tiles - 1, fields[1])
                    prepare(q + 1, x_b)
                else:
                    collect(q + (n - 1) // tiles, (n - 1) % tiles, fields[1 - n % 2])
                if n == tiles:
                    prepare(jnp.minimum(q + 2, steps - 1), x_a)
            return carry

        lax.fori_loop(0, response.shape[0] // 2, two, 0)
    collect(steps - 1, tiles - 1, fields[1])
    for k in range(3):
        for p in range(STEP):
            for j in range(strips.shape[0]):
                at = p * width + j * 128
                strips[j, pl.ds(p, steps, stride=STEP), :] = sums[k, :, at:at + 128]
        for j in range(strips.shape[0]):
            left = min(128, width - j * 128)
            out[k, :, j * 128:j * 128 + left] = strips[j, :, :left]


def local(cells, voltages, kernel_table, station_rows, station_cols, kernel_offset):
    times, chans = voltages.shape[1], voltages.shape[2]
    stations = station_rows.shape[0]
    variants, taps = kernel_table.shape[0], kernel_table.shape[1]
    count = lax.axis_size("chan")
    height = cells // count
    width = cells // lax.axis_size("row")
    here = lax.axis_index("chan")
    steps = height // STEP
    lanes = STEP * width
    planes = times * chans
    place = jnp.stack([here, here * height, lax.axis_index("row") * width]).astype(jnp.int32)
    vmem = pl.BlockSpec(memory_space=pltpu.VMEM)
    smem = pl.BlockSpec(memory_space=pltpu.SMEM)
    f32, bf16 = jnp.float32, jnp.bfloat16
    mib = 1024 * 1024

    bits = []
    while (1 << len(bits)) < count:
        bits.append(count >> (len(bits) + 1))
    own = voltages.transpose(0, 1, 3, 2).reshape(2 * times * voltages.shape[3], chans)
    held, blocks, masks, reach = own, [own], [(0,)], (0,)

    lines = [v.reshape(1, stations) for v in (station_rows, station_cols, kernel_offset)]
    make_tables = lambda held: pl.pallas_call(
        lambda *refs: table_kernel(cells, width, *refs),
        out_shape=[
            jax.ShapeDtypeStruct((stations, lanes), f32),
            jax.ShapeDtypeStruct((stations, lanes), f32),
            jax.ShapeDtypeStruct((stations, 128), jnp.int32),
            jax.ShapeDtypeStruct((steps, 8, lanes), f32),
            jax.ShapeDtypeStruct((steps, 8, lanes), f32),
            jax.ShapeDtypeStruct(held.shape, bf16),
        ],
        in_specs=[vmem, smem, vmem, vmem, vmem, vmem],
        out_specs=[vmem] * 6,
        compiler_params=pltpu.CompilerParams(vmem_limit_bytes=16 * mib),
        cost_estimate=pl.CostEstimate(flops=100 * stations * lanes, bytes_accessed=16 * stations * lanes, transcendentals=0),
    )(held, place, *lines, kernel_table.reshape(variants * taps, taps))

    ahead = steps // 4 * 2
    shares = [(0, steps - ahead), (steps - ahead, ahead)]
    responses = []
    for cut, bit in enumerate(bits):
        came = lax.ppermute(held, "chan", [(j, j ^ bit) for j in range(count)])
        if cut == 0:
            *tables, held = make_tables(held)
        elif cut <= len(shares):
            first, part = shares[cut - 1]
            response, held = pl.pallas_call(
                lambda *refs, first=first: response_kernel(first, *refs),
                out_shape=[
                    jax.ShapeDtypeStruct((part, 2 * stations, lanes), bf16),
                    jax.ShapeDtypeStruct(held.shape, bf16),
                ],
                in_specs=[vmem] * 6,
                out_specs=[vmem] * 2,
                compiler_params=pltpu.CompilerParams(vmem_limit_bytes=16 * mib),
                cost_estimate=pl.CostEstimate(
                    flops=16 * part * stations * lanes, bytes_accessed=4 * part * stations * lanes, transcendentals=0
                ),
            )(held, *tables)
            responses.append(response)
        blocks.append(came)
        masks.append(tuple(m ^ bit for m in reach))
        reach = reach + masks[-1]
        held = jnp.concatenate([held, came])

    x = (2.0 * np.arange(chans) + 1.0 - chans) / chans
    norm = [
        float(1.0 / np.sqrt(np.sum(x ** (2 * k))) / (times * stations * taps * taps) * (16.0 / chans) ** k)
        for k in range(3)
    ]
    groups = (len(blocks), len(responses))
    return pl.pallas_call(
        lambda *refs: image_kernel(cells, chans, width, norm, masks, groups, *refs),
        out_shape=jax.ShapeDtypeStruct((3, height, width), f32),
        in_specs=[smem] + [vmem] * (1 + sum(groups)),
        out_specs=vmem,
        scratch_shapes=[
            pltpu.VMEM((2 * times, stations, chans), f32),
            pltpu.VMEM((planes, stations), f32),
            pltpu.VMEM((planes, stations), f32),
            pltpu.VMEM((steps, stations), f32),
            pltpu.VMEM((steps, stations), f32),
            pltpu.VMEM((2 * planes, 2 * stations), bf16),
            pltpu.VMEM((2 * planes, 2 * stations), bf16),
            pltpu.VMEM((2 * planes, TILE), f32),
            pltpu.VMEM((2 * planes, TILE), f32),
            pltpu.VMEM((3, steps, lanes + 128), f32),
            pltpu.VMEM((-(-width // 128), height, 128), f32),
        ],
        compiler_params=pltpu.CompilerParams(vmem_limit_bytes=32 * mib),
        cost_estimate=pl.CostEstimate(
            flops=8 * steps * planes * stations * lanes, bytes_accessed=4 * steps * stations * lanes, transcendentals=0
        ),
    )(place, lines[0], *blocks, *responses)


def solution(mesh):
    cells = 768
    placed = (P(None, None, None, "chan"), P(), P(), P(), P())
    return jax.shard_map(
        lambda *args: local(cells, *args), mesh=mesh, in_specs=placed, out_specs=P(None, "chan", "row"), check_vma=False
    )
```

```python
import jax
import jax.numpy as jnp
import numpy as np
from jax import lax
from jax.experimental import pallas as pl
from jax.experimental.pallas import tpu as pltpu
from jax.sharding import PartitionSpec as P

TILE = 512
STEP = 8


def wave_fit(terms=7):
    nodes = 0.125 + 0.125 * np.cos(np.pi * (np.arange(200) + 0.5) / 200)
    root = np.sqrt(nodes)
    fit = np.polynomial.polynomial.polyfit
    cosine = fit(nodes, np.cos(2 * np.pi * root), terms - 1)
    sine = fit(nodes, np.sin(2 * np.pi * root) / root, terms - 1)
    return [float(c) for c in cosine], [float(c) for c in sine]


COS_FIT, SIN_FIT = wave_fit()


def horner(coefs, x):
    value = jnp.full_like(x, coefs[-1])
    for c in coefs[-2::-1]:
        value = value * x + c
    return value


def wave(product, cells):
    turns = product * (1.0 / cells)
    part = (product - cells * jnp.round(turns)) * (1.0 / cells)
    square = part * part
    return horner(COS_FIT, square), -part * horner(SIN_FIT, square)


def whole_of(shape, axis):
    return lax.broadcasted_iota(jnp.int32, shape, axis)


def split(value):
    high = value.astype(jnp.bfloat16)
    return high, (value - high.astype(jnp.float32)).astype(jnp.bfloat16)


def station_column(values, stations):
    return jnp.broadcast_to(values, (128, stations)).T


def table_kernel(
    cells, width, place, held_in, joined_in, table_in,
    base_re, base_im, pick, spread_re, spread_im, phase_re, phase_im, held, joined, table, arrived
):
    copies = [
        pltpu.make_async_copy(source, target, arrived.at[n])
        for n, (source, target) in enumerate((
            (joined_in, joined), (table_in, table), (held_in, held),
        ))
    ]
    for copy in copies:
        copy.start()
    for copy in copies:
        copy.wait()
    stations = joined.shape[1]
    steps, lanes = spread_re.shape[0], spread_re.shape[2]
    taps = table.shape[1]
    variants = table.shape[0] // taps
    first_row = place[1].astype(jnp.float32)
    first_col = place[2].astype(jnp.float32)
    code = joined[...].astype(jnp.float32)
    rows = jnp.floor((code + 0.5) * (1.0 / (cells * variants)))
    code = code - rows * float(cells * variants)
    cols = jnp.floor((code + 0.5) * (1.0 / variants))
    pick[...] = station_column(code - cols * float(variants), stations).astype(jnp.int32)
    row_of = station_column(rows, stations)
    col_of = station_column(cols, stations)
    start = first_row + float(STEP) * whole_of((steps, stations), 0).astype(jnp.float32)
    phase_re[...], phase_im[...] = wave(start * rows, cells)

    def down_across(shape, start):
        lane = whole_of(shape, 1) + start
        down = jnp.zeros(shape, jnp.float32)
        for p in range(1, STEP):
            down = jnp.where(lane >= p * width, float(p), down)
        return down, lane.astype(jnp.float32) - down * width + first_col

    half = lanes // 2
    leap_re, leap_im = wave(row_of * float(STEP // 2), cells)
    for tile in range(half // 128):
        at = slice(tile * 128, (tile + 1) * 128)
        later = slice(half + tile * 128, half + (tile + 1) * 128)
        down, across = down_across((stations, 128), tile * 128)
        real, imag = wave(row_of * down + col_of * across, cells)
        base_re[:, at], base_im[:, at] = real, imag
        base_re[:, later] = real * leap_re - imag * leap_im
        base_im[:, later] = real * leap_im + imag * leap_re

    down, across = down_across((taps, lanes), 0)
    tap = whole_of((taps, lanes), 0).astype(jnp.float32)
    kernels = table[...]

    def over_columns(value):
        high, low = split(value)
        return jnp.dot(kernels, high, preferred_element_type=jnp.float32) + jnp.dot(
            kernels, low, preferred_element_type=jnp.float32
        )

    half_re, half_im = [over_columns(value) for value in wave(tap * across, cells)]
    turn_re, turn_im = wave(tap * down, cells)
    tall = -(-steps // 16) * 16
    lane = whole_of((tall, 6 * taps), 1)
    start = first_row + float(STEP) * whole_of((tall, 6 * taps), 0).astype(jnp.float32)
    left_re, left_im = wave(start * (lane % taps).astype(jnp.float32), cells)
    value = jnp.where(lane // taps % 2 == 0, left_re, -left_im)
    high, low = split(value)
    left = jnp.where(lane // (2 * taps) == 1, low.astype(jnp.float32), high.astype(jnp.float32)).astype(jnp.bfloat16)
    for o in range(variants):
        rows_o = slice(o * taps, (o + 1) * taps)
        real = turn_re * half_re[rows_o] - turn_im * half_im[rows_o]
        imag = turn_re * half_im[rows_o] + turn_im * half_re[rows_o]
        for target, one, two in ((spread_re, real, imag), (spread_im, imag, -real)):
            one_high, one_low = split(one)
            two_high, two_low = split(two)
            right = jnp.concatenate([one_high, two_high, one_high, two_high, one_low, two_low], axis=0)
            target[:, o, :] = jnp.dot(left, right, preferred_element_type=jnp.float32)[:steps]


def response_kernel(first, held, base_re, base_im, pick, spread_re, spread_im, response, kept):
    kept[...] = held[...]
    parts, stations, lanes = response.shape[0], base_re.shape[0], base_re.shape[1]
    joint = 2 if parts % 2 == 0 else 1

    def some(i, carry):
        for tile in range(lanes // 128):
            at = slice(tile * 128, (tile + 1) * 128)
            tables = [
                (spread_re[first + joint * i + j, :, at], spread_im[first + joint * i + j, :, at]) for j in range(joint)
            ]
            for group in range(stations // 16):
                made = [([], []) for j in range(joint)]
                for half in range(2):
                    sub = slice(group * 16 + half * 8, group * 16 + half * 8 + 8)
                    index = pick[sub, :]
                    br = base_re[sub, at]
                    bi = base_im[sub, at]
                    for j in range(joint):
                        sr = jnp.take_along_axis(tables[j][0], index, axis=0)
                        si = jnp.take_along_axis(tables[j][1], index, axis=0)
                        made[j][0].append(br * sr - bi * si)
                        made[j][1].append(br * si + bi * sr)
                pair = slice(group * 16, group * 16 + 16)
                low = slice(stations + group * 16, stations + group * 16 + 16)
                for j in range(joint):
                    response[joint * i + j, pair, at] = jnp.concatenate(made[j][0], axis=0).astype(jnp.bfloat16)
                    response[joint * i + j, low, at] = jnp.concatenate(made[j][1], axis=0).astype(jnp.bfloat16)
        return carry

    lax.fori_loop(0, parts // joint, some, 0)


def image_kernel(
    chans, width, norm, masks, groups, place, phase_re, phase_im, *refs
):
    blocks, responses = refs[:groups[0]], refs[groups[0]:sum(groups)]
    out, turned, volt_re, volt_im, x_a, x_b, f_a, f_b, sums, strips = refs[sum(groups):]
    planes, stations = volt_re.shape
    steps, lanes = phase_re.shape[0], responses[0].shape[2]
    sheets = turned.shape[0]
    each = stations // len(sum(masks, ()))

    for block, held in zip(blocks, masks):
        value = block[...].astype(jnp.float32)
        for n, mask in enumerate(held):
            at = pl.multiple_of((place[0] ^ mask) * each, 8)
            for sheet in range(sheets):
                line = (n * sheets + sheet) * each
                turned[sheet, pl.ds(at, each), :] = value[line:line + each]
    for sheet in range(sheets):
        target = volt_re if sheet < sheets // 2 else volt_im
        at = sheet % (sheets // 2) * chans
        target[at:at + chans, :] = turned[sheet].T
    def prepare(q, x_out):
        pr = phase_re[pl.ds(q, 1), :]
        pi = phase_im[pl.ds(q, 1), :]
        vr = volt_re[...]
        vi = volt_im[...]
        xr = (vr * pr - vi * pi).astype(jnp.bfloat16)
        xi = (vr * pi + vi * pr).astype(jnp.bfloat16)
        x_out[:planes, :stations] = xr
        x_out[:planes, stations:] = -xi
        x_out[planes:, :stations] = xi
        x_out[planes:, stations:] = xr

    step_of = (2.0 * whole_of((8, TILE), 0).astype(jnp.float32) + 1.0 - chans) * 0.0625

    def collect(q, tile, field):
        zero = jnp.zeros((8, TILE), jnp.float32)
        s0, s1, s2 = zero, zero, zero
        for g in range(chans // 8 - 1, -1, -1):
            for t in range(2 * planes // chans):
                line = t * chans + g * 8
                part = field[line:line + 8, :]
                total = part * part if t == 0 else total + part * part
            s0 = s0 + total
            s1 = s1 + s0
            s2 = s2 + s1
        g1 = s1 - s0
        g2 = 2.0 * s2 - 3.0 * s1 + s0
        first = g1 + step_of * s0
        second = g2 + step_of * (2.0 * g1 + step_of * s0)
        for k, value in enumerate((s0, first, second)):
            sums[k, pl.ds(q, 1), tile * TILE:(tile + 1) * TILE] = norm[k] * jnp.sum(value, axis=0, keepdims=True)

    tiles = lanes // TILE
    fields = (f_a, f_b)
    xs = (x_a, x_b)
    prepare(0, x_a)
    f_b[...] = jnp.zeros_like(f_b)

    def chunk(q, turn, response, index):
        for n in range(tiles):
            side = (turn * tiles + n) % 2
            fields[side][...] = jnp.dot(
                xs[turn][...], response[index, :, n * TILE:(n + 1) * TILE], preferred_element_type=jnp.float32
            )
            if n == 0:
                collect(jnp.maximum(q - 1, 0), tiles - 1, fields[1 - side])
                prepare(jnp.minimum(q + 1, steps - 1), xs[1 - turn])
            else:
                collect(q, n - 1, fields[1 - side])

    base, turn = 0, 0
    for response in responses:
        here = response.shape[0]

        def two(i, carry):
            for j in range(2):
                chunk(base + 2 * i + j, (turn + j) % 2, response, 2 * i + j)
            return carry

        lax.fori_loop(0, here // 2, two, 0)
        if here % 2:
            chunk(base + here - 1, turn, response, here - 1)
        base, turn = base + here, (turn + here) % 2
    collect(steps - 1, tiles - 1, fields[(steps * tiles - 1) % 2])
    for k in range(3):
        for p in range(STEP):
            for j in range(strips.shape[0]):
                at = p * width + j * 128
                strips[j, pl.ds(p, steps, stride=STEP), :] = sums[k, :, at:at + 128]
        for j in range(strips.shape[0]):
            left = min(128, width - j * 128)
            out[k, :, j * 128:j * 128 + left] = strips[j, :, :left]


def local(cells, voltages, kernel_table, station_rows, station_cols, kernel_offset):
    times, chans = voltages.shape[1], voltages.shape[2]
    stations = station_rows.shape[0]
    variants, taps = kernel_table.shape[0], kernel_table.shape[1]
    count = lax.axis_size("chan")
    height = cells // count
    width = cells // lax.axis_size("row")
    here = lax.axis_index("chan")
    steps = height // STEP
    lanes = STEP * width
    planes = times * chans
    place = jnp.stack([here, here * height, lax.axis_index("row") * width]).astype(jnp.int32)
    vmem = pl.BlockSpec(memory_space=pltpu.VMEM)
    smem = pl.BlockSpec(memory_space=pltpu.SMEM)
    f32, bf16 = jnp.float32, jnp.bfloat16
    mib = 1024 * 1024

    bits = []
    while (1 << len(bits)) < count:
        bits.append(count >> (len(bits) + 1))
    hbm = pl.BlockSpec(memory_space=pltpu.HBM)
    joined = ((station_rows * cells + station_cols) * variants + kernel_offset).reshape(1, stations)
    own = voltages.transpose(0, 1, 3, 2).reshape(2 * times * voltages.shape[3], chans)
    *tables, phase_re, phase_im, held = pl.pallas_call(
        lambda *refs: table_kernel(cells, width, *refs),
        out_shape=[
            jax.ShapeDtypeStruct((stations, lanes), f32),
            jax.ShapeDtypeStruct((stations, lanes), f32),
            jax.ShapeDtypeStruct((stations, 128), jnp.int32),
            jax.ShapeDtypeStruct((steps, 8, lanes), f32),
            jax.ShapeDtypeStruct((steps, 8, lanes), f32),
            jax.ShapeDtypeStruct((steps, stations), f32),
            jax.ShapeDtypeStruct((steps, stations), f32),
            jax.ShapeDtypeStruct(own.shape, bf16),
        ],
        in_specs=[smem] + [hbm] * 3,
        out_specs=[vmem] * 8,
        scratch_shapes=[
            pltpu.VMEM((1, stations), jnp.int32),
            pltpu.VMEM((variants * taps, taps), bf16),
            pltpu.SemaphoreType.DMA((3,)),
        ],
        compiler_params=pltpu.CompilerParams(vmem_limit_bytes=16 * mib),
        cost_estimate=pl.CostEstimate(flops=100 * stations * lanes, bytes_accessed=16 * stations * lanes, transcendentals=0),
    )(place, own, joined, kernel_table.reshape(variants * taps, taps))

    blocks, masks, reach = [held], [(0,)], (0,)
    shares = [(k * (steps // 3), steps // 3) for k in range(2)]
    shares.append((steps // 3 * 2, steps - steps // 3 * 2))
    responses = []
    for cut, bit in enumerate(bits):
        came = lax.ppermute(held, "chan", [(j, j ^ bit) for j in range(count)])
        if cut < len(shares):
            first, part = shares[cut]
            response, held = pl.pallas_call(
                lambda *refs, first=first: response_kernel(first, *refs),
                out_shape=[
                    jax.ShapeDtypeStruct((part, 2 * stations, lanes), bf16),
                    jax.ShapeDtypeStruct(held.shape, bf16),
                ],
                in_specs=[vmem] * 6,
                out_specs=[vmem] * 2,
                compiler_params=pltpu.CompilerParams(vmem_limit_bytes=16 * mib),
                cost_estimate=pl.CostEstimate(
                    flops=16 * part * stations * lanes, bytes_accessed=4 * part * stations * lanes, transcendentals=0
                ),
            )(held, *tables)
            responses.append(response)
        blocks.append(came)
        masks.append(tuple(m ^ bit for m in reach))
        reach = reach + masks[-1]
        held = jnp.concatenate([held, came])

    x = (2.0 * np.arange(chans) + 1.0 - chans) / chans
    norm = [
        float(1.0 / np.sqrt(np.sum(x ** (2 * k))) / (times * stations * taps * taps) * (16.0 / chans) ** k)
        for k in range(3)
    ]
    groups = (len(blocks), len(responses))
    return pl.pallas_call(
        lambda *refs: image_kernel(chans, width, norm, masks, groups, *refs),
        out_shape=jax.ShapeDtypeStruct((3, height, width), f32),
        in_specs=[smem] + [vmem] * (2 + sum(groups)),
        out_specs=vmem,
        scratch_shapes=[
            pltpu.VMEM((2 * times, stations, chans), f32),
            pltpu.VMEM((planes, stations), f32),
            pltpu.VMEM((planes, stations), f32),
            pltpu.VMEM((2 * planes, 2 * stations), bf16),
            pltpu.VMEM((2 * planes, 2 * stations), bf16),
            pltpu.VMEM((2 * planes, TILE), f32),
            pltpu.VMEM((2 * planes, TILE), f32),
            pltpu.VMEM((3, steps, lanes + 128), f32),
            pltpu.VMEM((-(-width // 128), height, 128), f32),
        ],
        compiler_params=pltpu.CompilerParams(vmem_limit_bytes=32 * mib),
        cost_estimate=pl.CostEstimate(
            flops=8 * steps * planes * stations * lanes, bytes_accessed=4 * steps * stations * lanes, transcendentals=0
        ),
    )(place, phase_re, phase_im, *blocks, *responses)


def solution(mesh):
    cells = 768
    placed = (P(None, None, None, "chan"), P(), P(), P(), P())
    return jax.shard_map(
        lambda *args: local(cells, *args), mesh=mesh, in_specs=placed, out_specs=P(None, "chan", "row"), check_vma=False
    )
```

```python
import jax
import jax.numpy as jnp
import numpy as np
from jax import lax
from jax.experimental import pallas as pl
from jax.experimental.pallas import tpu as pltpu
from jax.sharding import PartitionSpec as P

TILE = 256
STEP = 8


def wave_fit(terms=7):
    nodes = 0.125 + 0.125 * np.cos(np.pi * (np.arange(200) + 0.5) / 200)
    root = np.sqrt(nodes)
    fit = np.polynomial.polynomial.polyfit
    cosine = fit(nodes, np.cos(2 * np.pi * root), terms - 1)
    sine = fit(nodes, np.sin(2 * np.pi * root) / root, terms - 1)
    return [float(c) for c in cosine], [float(c) for c in sine]


COS_FIT, SIN_FIT = wave_fit()


def horner(coefs, x):
    value = jnp.full_like(x, coefs[-1])
    for c in coefs[-2::-1]:
        value = value * x + c
    return value


def wave(product, cells):
    turns = product * (1.0 / cells)
    part = (product - cells * jnp.round(turns)) * (1.0 / cells)
    square = part * part
    return horner(COS_FIT, square), -part * horner(SIN_FIT, square)


def whole_of(shape, axis):
    return lax.broadcasted_iota(jnp.int32, shape, axis)


def split(value):
    high = value.astype(jnp.bfloat16)
    return high, (value - high.astype(jnp.float32)).astype(jnp.bfloat16)


def station_column(values, stations):
    return jnp.broadcast_to(values, (128, stations)).T


def table_kernel(
    cells, width, place, held_in, joined_in, table_in,
    base_re, base_im, pick, spread_re, spread_im, phase_re, phase_im, held, joined, table, arrived
):
    copies = [
        pltpu.make_async_copy(source, target, arrived.at[n])
        for n, (source, target) in enumerate((
            (joined_in, joined), (table_in, table), (held_in, held),
        ))
    ]
    for copy in copies:
        copy.start()
    for copy in copies:
        copy.wait()
    stations = joined.shape[1]
    steps, lanes = spread_re.shape[0], spread_re.shape[2]
    taps = table.shape[1]
    variants = table.shape[0] // taps
    first_row = place[1].astype(jnp.float32)
    first_col = place[2].astype(jnp.float32)
    code = joined[...].astype(jnp.float32)
    rows = jnp.floor((code + 0.5) * (1.0 / (cells * variants)))
    code = code - rows * float(cells * variants)
    cols = jnp.floor((code + 0.5) * (1.0 / variants))
    pick[...] = station_column(code - cols * float(variants), stations).astype(jnp.int32)
    row_of = station_column(rows, stations)
    col_of = station_column(cols, stations)
    start = first_row + float(STEP) * whole_of((steps, stations), 0).astype(jnp.float32)
    phase_re[...], phase_im[...] = wave(start * rows, cells)

    def down_across(shape, start):
        lane = whole_of(shape, 1) + start
        down = jnp.zeros(shape, jnp.float32)
        for p in range(1, STEP):
            down = jnp.where(lane >= p * width, float(p), down)
        return down, lane.astype(jnp.float32) - down * width + first_col

    half = lanes // 2
    leap_re, leap_im = wave(row_of * float(STEP // 2), cells)
    for tile in range(half // 128):
        at = slice(tile * 128, (tile + 1) * 128)
        later = slice(half + tile * 128, half + (tile + 1) * 128)
        down, across = down_across((stations, 128), tile * 128)
        real, imag = wave(row_of * down + col_of * across, cells)
        base_re[:, at], base_im[:, at] = real, imag
        base_re[:, later] = real * leap_re - imag * leap_im
        base_im[:, later] = real * leap_im + imag * leap_re

    down, across = down_across((taps, lanes), 0)
    tap = whole_of((taps, lanes), 0).astype(jnp.float32)
    kernels = table[...]

    def over_columns(value):
        high, low = split(value)
        return jnp.dot(kernels, high, preferred_element_type=jnp.float32) + jnp.dot(
            kernels, low, preferred_element_type=jnp.float32
        )

    half_re, half_im = [over_columns(value) for value in wave(tap * across, cells)]
    turn_re, turn_im = wave(tap * down, cells)
    tall = -(-steps // 16) * 16
    lane = whole_of((tall, 6 * taps), 1)
    start = first_row + float(STEP) * whole_of((tall, 6 * taps), 0).astype(jnp.float32)
    left_re, left_im = wave(start * (lane % taps).astype(jnp.float32), cells)
    value = jnp.where(lane // taps % 2 == 0, left_re, -left_im)
    high, low = split(value)
    left = jnp.where(lane // (2 * taps) == 1, low.astype(jnp.float32), high.astype(jnp.float32)).astype(jnp.bfloat16)
    for o in range(variants):
        rows_o = slice(o * taps, (o + 1) * taps)
        real = turn_re * half_re[rows_o] - turn_im * half_im[rows_o]
        imag = turn_re * half_im[rows_o] + turn_im * half_re[rows_o]
        for target, one, two in ((spread_re, real, imag), (spread_im, imag, -real)):
            one_high, one_low = split(one)
            two_high, two_low = split(two)
            right = jnp.concatenate([one_high, two_high, one_high, two_high, one_low, two_low], axis=0)
            target[:, o, :] = jnp.dot(left, right, preferred_element_type=jnp.float32)[:steps]


def response_kernel(first, held, base_re, base_im, pick, spread_re, spread_im, response, kept):
    kept[...] = held[...]
    parts, stations, lanes = response.shape[0], base_re.shape[0], base_re.shape[1]
    joint = 2 if parts % 2 == 0 else 1

    def some(i, carry):
        for tile in range(lanes // 128):
            at = slice(tile * 128, (tile + 1) * 128)
            tables = [
                (spread_re[first + joint * i + j, :, at], spread_im[first + joint * i + j, :, at]) for j in range(joint)
            ]
            for group in range(stations // 16):
                made = [([], []) for j in range(joint)]
                for half in range(2):
                    sub = slice(group * 16 + half * 8, group * 16 + half * 8 + 8)
                    index = pick[sub, :]
                    br = base_re[sub, at]
                    bi = base_im[sub, at]
                    for j in range(joint):
                        sr = jnp.take_along_axis(tables[j][0], index, axis=0)
                        si = jnp.take_along_axis(tables[j][1], index, axis=0)
                        made[j][0].append(br * sr - bi * si)
                        made[j][1].append(br * si + bi * sr)
                pair = slice(group * 16, group * 16 + 16)
                low = slice(stations + group * 16, stations + group * 16 + 16)
                for j in range(joint):
                    response[joint * i + j, pair, at] = jnp.concatenate(made[j][0], axis=0).astype(jnp.bfloat16)
                    response[joint * i + j, low, at] = jnp.concatenate(made[j][1], axis=0).astype(jnp.bfloat16)
        return carry

    lax.fori_loop(0, parts // joint, some, 0)


def image_kernel(
    chans, width, norm, masks, groups, place, phase_re, phase_im, *refs
):
    blocks, responses = refs[:groups[0]], refs[groups[0]:sum(groups)]
    out, turned, volt_re, volt_im, x_a, x_b, sums, strips = refs[sum(groups):]
    planes, stations = volt_re.shape
    steps, lanes = phase_re.shape[0], responses[0].shape[2]
    sheets = turned.shape[0]
    each = stations // len(sum(masks, ()))

    for block, held in zip(blocks, masks):
        value = block[...].astype(jnp.float32)
        for n, mask in enumerate(held):
            at = pl.multiple_of((place[0] ^ mask) * each, 8)
            for sheet in range(sheets):
                line = (n * sheets + sheet) * each
                turned[sheet, pl.ds(at, each), :] = value[line:line + each]
    times = sheets // 2
    for sheet in range(sheets):
        target = volt_re if sheet < times else volt_im
        facing = turned[sheet].T
        for g in range(chans // 8):
            at = (g * times + sheet % times) * 8
            target[at:at + 8, :] = facing[g * 8:g * 8 + 8]
    span = 8 * times

    def prepare(q, x_out):
        pr = phase_re[pl.ds(q, 1), :]
        pi = phase_im[pl.ds(q, 1), :]
        for g in range(chans // 8):
            vr = volt_re[g * span:(g + 1) * span, :]
            vi = volt_im[g * span:(g + 1) * span, :]
            xr = (vr * pr - vi * pi).astype(jnp.bfloat16)
            xi = (vr * pi + vi * pr).astype(jnp.bfloat16)
            real = slice(2 * g * span, (2 * g + 1) * span)
            imag = slice((2 * g + 1) * span, (2 * g + 2) * span)
            x_out[real, :stations] = xr
            x_out[real, stations:] = -xi
            x_out[imag, :stations] = xi
            x_out[imag, stations:] = xr

    top = chans // 8
    step_of = top + (2.0 * whole_of((8, TILE), 0).astype(jnp.float32) + 1.0 - chans) * 0.0625

    def collect(q, tile, field):
        s0, s1, s2 = None, None, None
        for g in range(top):
            for t in range(2 * times):
                line = (g * 2 * times + t) * 8
                part = field[line:line + 8, :]
                total = part * part if t == 0 else total + part * part
            s0 = total if g == 0 else s0 + total
            s1 = s0 if g == 0 else s1 + s0
            s2 = s1 if g == 0 else s2 + s1
        first = step_of * s0 - s1
        second = step_of * (step_of * s0 - 2.0 * s1) + (2.0 * s2 - s1)
        for k, value in enumerate((s0, first, second)):
            sums[k, pl.ds(q, 1), tile * TILE:(tile + 1) * TILE] = norm[k] * jnp.sum(value, axis=0, keepdims=True)

    tiles = lanes // TILE
    xs = (x_a, x_b)
    prepare(0, x_a)

    def chunk(q, turn, response, index):
        for n in range(tiles):
            field = jnp.dot(
                xs[turn][...], response[index, :, n * TILE:(n + 1) * TILE], preferred_element_type=jnp.float32
            )
            if n == 0:
                prepare(jnp.minimum(q + 1, steps - 1), xs[1 - turn])
            collect(q, n, field)

    base, turn = 0, 0
    for response in responses:
        here = response.shape[0]

        def two(i, carry):
            for j in range(2):
                chunk(base + 2 * i + j, (turn + j) % 2, response, 2 * i + j)
            return carry

        lax.fori_loop(0, here // 2, two, 0)
        if here % 2:
            chunk(base + here - 1, turn, response, here - 1)
        base, turn = base + here, (turn + here) % 2
    for k in range(3):
        for p in range(STEP):
            for j in range(strips.shape[0]):
                at = p * width + j * 128
                strips[j, pl.ds(p, steps, stride=STEP), :] = sums[k, :, at:at + 128]
        for j in range(strips.shape[0]):
            left = min(128, width - j * 128)
            out[k, :, j * 128:j * 128 + left] = strips[j, :, :left]


def local(cells, voltages, kernel_table, station_rows, station_cols, kernel_offset):
    times, chans = voltages.shape[1], voltages.shape[2]
    stations = station_rows.shape[0]
    variants, taps = kernel_table.shape[0], kernel_table.shape[1]
    count = lax.axis_size("chan")
    height = cells // count
    width = cells // lax.axis_size("row")
    here = lax.axis_index("chan")
    steps = height // STEP
    lanes = STEP * width
    planes = times * chans
    place = jnp.stack([here, here * height, lax.axis_index("row") * width]).astype(jnp.int32)
    vmem = pl.BlockSpec(memory_space=pltpu.VMEM)
    smem = pl.BlockSpec(memory_space=pltpu.SMEM)
    f32, bf16 = jnp.float32, jnp.bfloat16
    mib = 1024 * 1024

    bits = []
    while (1 << len(bits)) < count:
        bits.append(count >> (len(bits) + 1))
    hbm = pl.BlockSpec(memory_space=pltpu.HBM)
    joined = ((station_rows * cells + station_cols) * variants + kernel_offset).reshape(1, stations)
    own = voltages.transpose(0, 1, 3, 2).reshape(2 * times * voltages.shape[3], chans)
    make_tables = lambda: pl.pallas_call(
        lambda *refs: table_kernel(cells, width, *refs),
        out_shape=[
            jax.ShapeDtypeStruct((stations, lanes), f32),
            jax.ShapeDtypeStruct((stations, lanes), f32),
            jax.ShapeDtypeStruct((stations, 128), jnp.int32),
            jax.ShapeDtypeStruct((steps, 8, lanes), f32),
            jax.ShapeDtypeStruct((steps, 8, lanes), f32),
            jax.ShapeDtypeStruct((steps, stations), f32),
            jax.ShapeDtypeStruct((steps, stations), f32),
            jax.ShapeDtypeStruct(own.shape, bf16),
        ],
        in_specs=[smem] + [hbm] * 3,
        out_specs=[vmem] * 8,
        scratch_shapes=[
            pltpu.VMEM((1, stations), jnp.int32),
            pltpu.VMEM((variants * taps, taps), bf16),
            pltpu.SemaphoreType.DMA((3,)),
        ],
        compiler_params=pltpu.CompilerParams(vmem_limit_bytes=16 * mib),
        cost_estimate=pl.CostEstimate(flops=100 * stations * lanes, bytes_accessed=16 * stations * lanes, transcendentals=0),
    )(place, own, joined, kernel_table.reshape(variants * taps, taps))

    ahead = steps // 2
    shares = [(0, steps - ahead), (steps - ahead, ahead)]
    held, reach, responses = own, (0,), []
    for cut, bit in enumerate(bits):
        came = lax.ppermute(held, "chan", [(j, j ^ bit) for j in range(count)])
        if cut == 0:
            *tables, phase_re, phase_im, held = make_tables()
        elif cut <= len(shares):
            first, part = shares[cut - 1]
            response, held = pl.pallas_call(
                lambda *refs, first=first: response_kernel(first, *refs),
                out_shape=[
                    jax.ShapeDtypeStruct((part, 2 * stations, lanes), bf16),
                    jax.ShapeDtypeStruct(held.shape, bf16),
                ],
                in_specs=[vmem] * 6,
                out_specs=[vmem] * 2,
                compiler_params=pltpu.CompilerParams(vmem_limit_bytes=16 * mib),
                cost_estimate=pl.CostEstimate(
                    flops=16 * part * stations * lanes, bytes_accessed=4 * part * stations * lanes, transcendentals=0
                ),
            )(held, *tables)
            responses.append(response)
        masks = [reach, tuple(m ^ bit for m in reach)]
        reach = sum(masks, ())
        blocks = [held, came]
        held = jnp.concatenate(blocks)

    x = (2.0 * np.arange(chans) + 1.0 - chans) / chans
    norm = [
        float(1.0 / np.sqrt(np.sum(x ** (2 * k))) / (times * stations * taps * taps) * (16.0 / chans) ** k)
        for k in range(3)
    ]
    groups = (len(blocks), len(responses))
    return pl.pallas_call(
        lambda *refs: image_kernel(chans, width, norm, masks, groups, *refs),
        out_shape=jax.ShapeDtypeStruct((3, height, width), f32),
        in_specs=[smem] + [vmem] * (2 + sum(groups)),
        out_specs=vmem,
        scratch_shapes=[
            pltpu.VMEM((2 * times, stations, chans), f32),
            pltpu.VMEM((planes, stations), f32),
            pltpu.VMEM((planes, stations), f32),
            pltpu.VMEM((2 * planes, 2 * stations), bf16),
            pltpu.VMEM((2 * planes, 2 * stations), bf16),
            pltpu.VMEM((3, steps, lanes + 128), f32),
            pltpu.VMEM((-(-width // 128), height, 128), f32),
        ],
        compiler_params=pltpu.CompilerParams(vmem_limit_bytes=32 * mib),
        cost_estimate=pl.CostEstimate(
            flops=8 * steps * planes * stations * lanes, bytes_accessed=4 * steps * stations * lanes, transcendentals=0
        ),
    )(place, phase_re, phase_im, *blocks, *responses)


def solution(mesh):
    cells = 768
    placed = (P(None, None, None, "chan"), P(), P(), P(), P())
    return jax.shard_map(
        lambda *args: local(cells, *args), mesh=mesh, in_specs=placed, out_specs=P(None, "chan", "row"), check_vma=False
    )
```

```python
import jax
import jax.numpy as jnp
import numpy as np
from jax import lax
from jax.experimental import pallas as pl
from jax.experimental.pallas import tpu as pltpu
from jax.sharding import PartitionSpec as P

TILE = 512
STEP = 8


def wave_fit(terms=7):
    nodes = 0.125 + 0.125 * np.cos(np.pi * (np.arange(200) + 0.5) / 200)
    root = np.sqrt(nodes)
    fit = np.polynomial.polynomial.polyfit
    cosine = fit(nodes, np.cos(2 * np.pi * root), terms - 1)
    sine = fit(nodes, np.sin(2 * np.pi * root) / root, terms - 1)
    return [float(c) for c in cosine], [float(c) for c in sine]


COS_FIT, SIN_FIT = wave_fit()


def horner(coefs, x):
    value = jnp.full_like(x, coefs[-1])
    for c in coefs[-2::-1]:
        value = value * x + c
    return value


def wave(product, cells):
    turns = product * (1.0 / cells)
    part = (product - cells * jnp.round(turns)) * (1.0 / cells)
    square = part * part
    return horner(COS_FIT, square), -part * horner(SIN_FIT, square)


def whole_of(shape, axis):
    return lax.broadcasted_iota(jnp.int32, shape, axis)


def split(value):
    high = value.astype(jnp.bfloat16)
    return high, (value - high.astype(jnp.float32)).astype(jnp.bfloat16)


def station_column(values, stations):
    return jnp.broadcast_to(values, (128, stations)).T


def table_kernel(
    cells, width, place, held_in, joined_in, table_in,
    base_re, base_im, pick, spread_re, spread_im, phase_re, phase_im, held, joined, table, arrived
):
    copies = [
        pltpu.make_async_copy(source, target, arrived.at[n])
        for n, (source, target) in enumerate((
            (joined_in, joined), (table_in, table), (held_in, held),
        ))
    ]
    for copy in copies:
        copy.start()
    for copy in copies:
        copy.wait()
    stations = joined.shape[1]
    steps, lanes = spread_re.shape[0], spread_re.shape[2]
    taps = table.shape[1]
    variants = table.shape[0] // taps
    first_row = place[1].astype(jnp.float32)
    first_col = place[2].astype(jnp.float32)
    code = joined[...].astype(jnp.float32)
    rows = jnp.floor((code + 0.5) * (1.0 / (cells * variants)))
    code = code - rows * float(cells * variants)
    cols = jnp.floor((code + 0.5) * (1.0 / variants))
    pick[...] = station_column(code - cols * float(variants), stations).astype(jnp.int32)
    row_of = station_column(rows, stations)
    col_of = station_column(cols, stations)
    start = first_row + float(STEP) * whole_of((steps, stations), 0).astype(jnp.float32)
    phase_re[...], phase_im[...] = wave(start * rows, cells)

    def down_across(shape, start):
        lane = whole_of(shape, 1) + start
        down = jnp.zeros(shape, jnp.float32)
        for p in range(1, STEP):
            down = jnp.where(lane >= p * width, float(p), down)
        return down, lane.astype(jnp.float32) - down * width + first_col

    half = lanes // 2
    leap_re, leap_im = wave(row_of * float(STEP // 2), cells)
    for tile in range(half // 128):
        at = slice(tile * 128, (tile + 1) * 128)
        later = slice(half + tile * 128, half + (tile + 1) * 128)
        down, across = down_across((stations, 128), tile * 128)
        real, imag = wave(row_of * down + col_of * across, cells)
        base_re[:, at], base_im[:, at] = real, imag
        base_re[:, later] = real * leap_re - imag * leap_im
        base_im[:, later] = real * leap_im + imag * leap_re

    down, across = down_across((taps, lanes), 0)
    tap = whole_of((taps, lanes), 0).astype(jnp.float32)
    kernels = table[...]

    def over_columns(value):
        high, low = split(value)
        return jnp.dot(kernels, high, preferred_element_type=jnp.float32) + jnp.dot(
            kernels, low, preferred_element_type=jnp.float32
        )

    half_re, half_im = [over_columns(value) for value in wave(tap * across, cells)]
    turn_re, turn_im = wave(tap * down, cells)
    tall = -(-steps // 16) * 16
    lane = whole_of((tall, 6 * taps), 1)
    start = first_row + float(STEP) * whole_of((tall, 6 * taps), 0).astype(jnp.float32)
    left_re, left_im = wave(start * (lane % taps).astype(jnp.float32), cells)
    value = jnp.where(lane // taps % 2 == 0, left_re, -left_im)
    high, low = split(value)
    left = jnp.where(lane // (2 * taps) == 1, low.astype(jnp.float32), high.astype(jnp.float32)).astype(jnp.bfloat16)
    for o in range(variants):
        rows_o = slice(o * taps, (o + 1) * taps)
        real = turn_re * half_re[rows_o] - turn_im * half_im[rows_o]
        imag = turn_re * half_im[rows_o] + turn_im * half_re[rows_o]
        for target, one, two in ((spread_re, real, imag), (spread_im, imag, -real)):
            one_high, one_low = split(one)
            two_high, two_low = split(two)
            right = jnp.concatenate([one_high, two_high, one_high, two_high, one_low, two_low], axis=0)
            target[:, o, :] = jnp.dot(left, right, preferred_element_type=jnp.float32)[:steps]


def response_kernel(first, held, base_re, base_im, pick, spread_re, spread_im, response, kept):
    kept[...] = held[...]
    parts, stations, lanes = response.shape[0], base_re.shape[0], base_re.shape[1]
    joint = 2 if parts % 2 == 0 else 1

    def some(i, carry):
        for tile in range(lanes // 128):
            at = slice(tile * 128, (tile + 1) * 128)
            tables = [
                (spread_re[first + joint * i + j, :, at], spread_im[first + joint * i + j, :, at]) for j in range(joint)
            ]
            for group in range(stations // 16):
                made = [([], []) for j in range(joint)]
                for half in range(2):
                    sub = slice(group * 16 + half * 8, group * 16 + half * 8 + 8)
                    index = pick[sub, :]
                    br = base_re[sub, at]
                    bi = base_im[sub, at]
                    for j in range(joint):
                        sr = jnp.take_along_axis(tables[j][0], index, axis=0)
                        si = jnp.take_along_axis(tables[j][1], index, axis=0)
                        made[j][0].append(br * sr - bi * si)
                        made[j][1].append(br * si + bi * sr)
                pair = slice(group * 16, group * 16 + 16)
                low = slice(stations + group * 16, stations + group * 16 + 16)
                for j in range(joint):
                    response[joint * i + j, pair, at] = jnp.concatenate(made[j][0], axis=0).astype(jnp.bfloat16)
                    response[joint * i + j, low, at] = jnp.concatenate(made[j][1], axis=0).astype(jnp.bfloat16)
        return carry

    lax.fori_loop(0, parts // joint, some, 0)


def image_kernel(
    chans, width, norm, masks, groups, place, phase_re, phase_im, *refs
):
    blocks, responses = refs[:groups[0]], refs[groups[0]:sum(groups)]
    out, turned, volt_re, volt_im, x_a, x_b, sums, strips = refs[sum(groups):]
    planes, stations = volt_re.shape
    steps, lanes = phase_re.shape[0], responses[0].shape[2]
    sheets = turned.shape[0]
    each = stations // len(sum(masks, ()))

    for block, held in zip(blocks, masks):
        value = block[...].astype(jnp.float32)
        for n, mask in enumerate(held):
            at = pl.multiple_of((place[0] ^ mask) * each, 8)
            for sheet in range(sheets):
                line = (n * sheets + sheet) * each
                turned[sheet, pl.ds(at, each), :] = value[line:line + each]
    times = sheets // 2
    for sheet in range(sheets):
        target = volt_re if sheet < times else volt_im
        facing = turned[sheet].T
        for g in range(chans // 8):
            at = (g * times + sheet % times) * 8
            target[at:at + 8, :] = facing[g * 8:g * 8 + 8]
    span = 8 * times

    def prepare(q, x_out):
        pr = phase_re[pl.ds(q, 1), :]
        pi = phase_im[pl.ds(q, 1), :]
        for g in range(chans // 8):
            vr = volt_re[g * span:(g + 1) * span, :]
            vi = volt_im[g * span:(g + 1) * span, :]
            xr = (vr * pr - vi * pi).astype(jnp.bfloat16)
            xi = (vr * pi + vi * pr).astype(jnp.bfloat16)
            real = slice(2 * g * span, (2 * g + 1) * span)
            imag = slice((2 * g + 1) * span, (2 * g + 2) * span)
            x_out[real, :stations] = xr
            x_out[real, stations:] = -xi
            x_out[imag, :stations] = xi
            x_out[imag, stations:] = xr

    top = chans // 8
    step_of = top + (2.0 * whole_of((8, TILE), 0).astype(jnp.float32) + 1.0 - chans) * 0.0625

    def collect(q, tile, field):
        s0, s1, s2 = None, None, None
        for g in range(top):
            for t in range(2 * times):
                line = (g * 2 * times + t) * 8
                part = field[line:line + 8, :]
                total = part * part if t == 0 else total + part * part
            s0 = total if g == 0 else s0 + total
            s1 = s0 if g == 0 else s1 + s0
            s2 = s1 if g == 0 else s2 + s1
        first = step_of * s0 - s1
        second = step_of * (step_of * s0 - 2.0 * s1) + (2.0 * s2 - s1)
        for k, value in enumerate((s0, first, second)):
            sums[k, pl.ds(q, 1), tile * TILE:(tile + 1) * TILE] = norm[k] * jnp.sum(value, axis=0, keepdims=True)

    tiles = lanes // TILE
    xs = (x_a, x_b)
    prepare(0, x_a)

    def chunk(q, turn, response, index):
        for n in range(tiles):
            field = jnp.dot(
                xs[turn][...], response[index, :, n * TILE:(n + 1) * TILE], preferred_element_type=jnp.float32
            )
            if n == 0:
                prepare(jnp.minimum(q + 1, steps - 1), xs[1 - turn])
            collect(q, n, field)

    base, turn = 0, 0
    for response in responses:
        here = response.shape[0]

        def two(i, carry):
            for j in range(2):
                chunk(base + 2 * i + j, (turn + j) % 2, response, 2 * i + j)
            return carry

        lax.fori_loop(0, here // 2, two, 0)
        if here % 2:
            chunk(base + here - 1, turn, response, here - 1)
        base, turn = base + here, (turn + here) % 2
    for k in range(3):
        for p in range(STEP):
            for j in range(strips.shape[0]):
                at = p * width + j * 128
                strips[j, pl.ds(p, steps, stride=STEP), :] = sums[k, :, at:at + 128]
        for j in range(strips.shape[0]):
            left = min(128, width - j * 128)
            out[k, :, j * 128:j * 128 + left] = strips[j, :, :left]


def local(cells, voltages, kernel_table, station_rows, station_cols, kernel_offset):
    times, chans = voltages.shape[1], voltages.shape[2]
    stations = station_rows.shape[0]
    variants, taps = kernel_table.shape[0], kernel_table.shape[1]
    count = lax.axis_size("chan")
    height = cells // count
    width = cells // lax.axis_size("row")
    here = lax.axis_index("chan")
    steps = height // STEP
    lanes = STEP * width
    planes = times * chans
    place = jnp.stack([here, here * height, lax.axis_index("row") * width]).astype(jnp.int32)
    vmem = pl.BlockSpec(memory_space=pltpu.VMEM)
    smem = pl.BlockSpec(memory_space=pltpu.SMEM)
    f32, bf16 = jnp.float32, jnp.bfloat16
    mib = 1024 * 1024

    bits = []
    while (1 << len(bits)) < count:
        bits.append(count >> (len(bits) + 1))
    hbm = pl.BlockSpec(memory_space=pltpu.HBM)
    joined = ((station_rows * cells + station_cols) * variants + kernel_offset).reshape(1, stations)
    own = voltages.transpose(0, 1, 3, 2).reshape(2 * times * voltages.shape[3], chans)
    make_tables = lambda: pl.pallas_call(
        lambda *refs: table_kernel(cells, width, *refs),
        out_shape=[
            jax.ShapeDtypeStruct((stations, lanes), f32),
            jax.ShapeDtypeStruct((stations, lanes), f32),
            jax.ShapeDtypeStruct((stations, 128), jnp.int32),
            jax.ShapeDtypeStruct((steps, 8, lanes), f32),
            jax.ShapeDtypeStruct((steps, 8, lanes), f32),
            jax.ShapeDtypeStruct((steps, stations), f32),
            jax.ShapeDtypeStruct((steps, stations), f32),
            jax.ShapeDtypeStruct(own.shape, bf16),
        ],
        in_specs=[smem] + [hbm] * 3,
        out_specs=[vmem] * 8,
        scratch_shapes=[
            pltpu.VMEM((1, stations), jnp.int32),
            pltpu.VMEM((variants * taps, taps), bf16),
            pltpu.SemaphoreType.DMA((3,)),
        ],
        compiler_params=pltpu.CompilerParams(vmem_limit_bytes=16 * mib),
        cost_estimate=pl.CostEstimate(flops=100 * stations * lanes, bytes_accessed=16 * stations * lanes, transcendentals=0),
    )(place, own, joined, kernel_table.reshape(variants * taps, taps))

    ahead = steps // 2
    shares = [(0, steps - ahead), (steps - ahead, ahead)]
    held, reach, responses = own, (0,), []
    for cut, bit in enumerate(bits):
        came = lax.ppermute(held, "chan", [(j, j ^ bit) for j in range(count)])
        if cut == 0:
            *tables, phase_re, phase_im, held = make_tables()
        elif cut <= len(shares):
            first, part = shares[cut - 1]
            response, held = pl.pallas_call(
                lambda *refs, first=first: response_kernel(first, *refs),
                out_shape=[
                    jax.ShapeDtypeStruct((part, 2 * stations, lanes), bf16),
                    jax.ShapeDtypeStruct(held.shape, bf16),
                ],
                in_specs=[vmem] * 6,
                out_specs=[vmem] * 2,
                compiler_params=pltpu.CompilerParams(vmem_limit_bytes=16 * mib),
                cost_estimate=pl.CostEstimate(
                    flops=16 * part * stations * lanes, bytes_accessed=4 * part * stations * lanes, transcendentals=0
                ),
            )(held, *tables)
            responses.append(response)
        masks = [reach, tuple(m ^ bit for m in reach)]
        reach = sum(masks, ())
        blocks = [held, came]
        held = jnp.concatenate(blocks)

    x = (2.0 * np.arange(chans) + 1.0 - chans) / chans
    norm = [
        float(1.0 / np.sqrt(np.sum(x ** (2 * k))) / (times * stations * taps * taps) * (16.0 / chans) ** k)
        for k in range(3)
    ]
    groups = (len(blocks), len(responses))
    return pl.pallas_call(
        lambda *refs: image_kernel(chans, width, norm, masks, groups, *refs),
        out_shape=jax.ShapeDtypeStruct((3, height, width), f32),
        in_specs=[smem] + [vmem] * (2 + sum(groups)),
        out_specs=vmem,
        scratch_shapes=[
            pltpu.VMEM((2 * times, stations, chans), f32),
            pltpu.VMEM((planes, stations), f32),
            pltpu.VMEM((planes, stations), f32),
            pltpu.VMEM((2 * planes, 2 * stations), bf16),
            pltpu.VMEM((2 * planes, 2 * stations), bf16),
            pltpu.VMEM((3, steps, lanes + 128), f32),
            pltpu.VMEM((-(-width // 128), height, 128), f32),
        ],
        compiler_params=pltpu.CompilerParams(vmem_limit_bytes=32 * mib),
        cost_estimate=pl.CostEstimate(
            flops=8 * steps * planes * stations * lanes, bytes_accessed=4 * steps * stations * lanes, transcendentals=0
        ),
    )(place, phase_re, phase_im, *blocks, *responses)


def solution(mesh):
    cells = 768
    placed = (P(None, None, None, "chan"), P(), P(), P(), P())
    return jax.shard_map(
        lambda *args: local(cells, *args), mesh=mesh, in_specs=placed, out_specs=P(None, "chan", "row"), check_vma=False
    )
```

```python
import jax
import jax.numpy as jnp
import numpy as np
from jax import lax
from jax.experimental import pallas as pl
from jax.experimental.pallas import tpu as pltpu
from jax.sharding import PartitionSpec as P

TILE = 512
STEP = 8


def wave_fit(terms=7):
    nodes = 0.125 + 0.125 * np.cos(np.pi * (np.arange(200) + 0.5) / 200)
    root = np.sqrt(nodes)
    fit = np.polynomial.polynomial.polyfit
    cosine = fit(nodes, np.cos(2 * np.pi * root), terms - 1)
    sine = fit(nodes, np.sin(2 * np.pi * root) / root, terms - 1)
    return [float(c) for c in cosine], [float(c) for c in sine]


COS_FIT, SIN_FIT = wave_fit()


def horner(coefs, x):
    value = jnp.full_like(x, coefs[-1])
    for c in coefs[-2::-1]:
        value = value * x + c
    return value


def wave(product, cells):
    turns = product * (1.0 / cells)
    part = (product - cells * jnp.round(turns)) * (1.0 / cells)
    square = part * part
    return horner(COS_FIT, square), -part * horner(SIN_FIT, square)


def whole_of(shape, axis):
    return lax.broadcasted_iota(jnp.int32, shape, axis)


def split(value):
    high = value.astype(jnp.bfloat16)
    return high, (value - high.astype(jnp.float32)).astype(jnp.bfloat16)


def station_column(values, stations):
    return jnp.broadcast_to(values, (128, stations)).T


def table_kernel(
    cells, width, place, joined_in, table_in,
    base_re, base_im, pick, spread_re, spread_im, phase_re, phase_im, joined, table, arrived
):
    copies = [
        pltpu.make_async_copy(source, target, arrived.at[n])
        for n, (source, target) in enumerate((
            (joined_in, joined), (table_in, table),
        ))
    ]
    for copy in copies:
        copy.start()
    for copy in copies:
        copy.wait()
    stations = joined.shape[1]
    steps, lanes = spread_re.shape[0], spread_re.shape[2]
    taps = table.shape[1]
    variants = table.shape[0] // taps
    first_row = place[1].astype(jnp.float32)
    first_col = place[2].astype(jnp.float32)
    code = joined[...].astype(jnp.float32)
    rows = jnp.floor((code + 0.5) * (1.0 / (cells * variants)))
    code = code - rows * float(cells * variants)
    cols = jnp.floor((code + 0.5) * (1.0 / variants))
    pick[...] = station_column(code - cols * float(variants), stations).astype(jnp.int32)
    row_of = station_column(rows, stations)
    col_of = station_column(cols, stations)
    start = first_row + float(STEP) * whole_of((steps, stations), 0).astype(jnp.float32)
    phase_re[...], phase_im[...] = wave(start * rows, cells)

    def down_across(shape, start):
        lane = whole_of(shape, 1) + start
        down = jnp.zeros(shape, jnp.float32)
        for p in range(1, STEP):
            down = jnp.where(lane >= p * width, float(p), down)
        return down, lane.astype(jnp.float32) - down * width + first_col

    half = lanes // 2
    leap_re, leap_im = wave(row_of * float(STEP // 2), cells)
    for tile in range(half // 128):
        at = slice(tile * 128, (tile + 1) * 128)
        later = slice(half + tile * 128, half + (tile + 1) * 128)
        down, across = down_across((stations, 128), tile * 128)
        real, imag = wave(row_of * down + col_of * across, cells)
        base_re[:, at], base_im[:, at] = real, imag
        base_re[:, later] = real * leap_re - imag * leap_im
        base_im[:, later] = real * leap_im + imag * leap_re

    down, across = down_across((taps, lanes), 0)
    tap = whole_of((taps, lanes), 0).astype(jnp.float32)
    kernels = table[...]

    def over_columns(value):
        high, low = split(value)
        return jnp.dot(kernels, high, preferred_element_type=jnp.float32) + jnp.dot(
            kernels, low, preferred_element_type=jnp.float32
        )

    half_re, half_im = [over_columns(value) for value in wave(tap * across, cells)]
    turn_re, turn_im = wave(tap * down, cells)
    tall = -(-steps // 16) * 16
    lane = whole_of((tall, 6 * taps), 1)
    start = first_row + float(STEP) * whole_of((tall, 6 * taps), 0).astype(jnp.float32)
    left_re, left_im = wave(start * (lane % taps).astype(jnp.float32), cells)
    value = jnp.where(lane // taps % 2 == 0, left_re, -left_im)
    high, low = split(value)
    left = jnp.where(lane // (2 * taps) == 1, low.astype(jnp.float32), high.astype(jnp.float32)).astype(jnp.bfloat16)
    for o in range(variants):
        rows_o = slice(o * taps, (o + 1) * taps)
        real = turn_re * half_re[rows_o] - turn_im * half_im[rows_o]
        imag = turn_re * half_im[rows_o] + turn_im * half_re[rows_o]
        for target, one, two in ((spread_re, real, imag), (spread_im, imag, -real)):
            one_high, one_low = split(one)
            two_high, two_low = split(two)
            right = jnp.concatenate([one_high, two_high, one_high, two_high, one_low, two_low], axis=0)
            target[:, o, :] = jnp.dot(left, right, preferred_element_type=jnp.float32)[:steps]


def response_kernel(first, base_re, base_im, pick, spread_re, spread_im, response):
    parts, stations, lanes = response.shape[0], base_re.shape[0], base_re.shape[1]
    joint = 2 if parts % 2 == 0 else 1

    def some(i, carry):
        for tile in range(lanes // 128):
            at = slice(tile * 128, (tile + 1) * 128)
            tables = [
                (spread_re[first + joint * i + j, :, at], spread_im[first + joint * i + j, :, at]) for j in range(joint)
            ]
            for group in range(stations // 16):
                made = [([], []) for j in range(joint)]
                for half in range(2):
                    sub = slice(group * 16 + half * 8, group * 16 + half * 8 + 8)
                    index = pick[sub, :]
                    br = base_re[sub, at]
                    bi = base_im[sub, at]
                    for j in range(joint):
                        sr = jnp.take_along_axis(tables[j][0], index, axis=0)
                        si = jnp.take_along_axis(tables[j][1], index, axis=0)
                        made[j][0].append(br * sr - bi * si)
                        made[j][1].append(br * si + bi * sr)
                pair = slice(group * 16, group * 16 + 16)
                low = slice(stations + group * 16, stations + group * 16 + 16)
                for j in range(joint):
                    response[joint * i + j, pair, at] = jnp.concatenate(made[j][0], axis=0).astype(jnp.bfloat16)
                    response[joint * i + j, low, at] = jnp.concatenate(made[j][1], axis=0).astype(jnp.bfloat16)
        return carry

    lax.fori_loop(0, parts // joint, some, 0)


def image_kernel(
    chans, width, norm, masks, groups, place, phase_re, phase_im, *refs
):
    blocks, responses = refs[:groups[0]], refs[groups[0]:sum(groups)]
    out, turned, volt_re, volt_im, x_a, x_b, sums, strips = refs[sum(groups):]
    planes, stations = volt_re.shape
    steps, lanes = phase_re.shape[0], responses[0].shape[2]
    sheets = turned.shape[0]
    each = stations // len(sum(masks, ()))

    for block, held in zip(blocks, masks):
        value = block[...].astype(jnp.float32)
        for n, mask in enumerate(held):
            at = pl.multiple_of((place[0] ^ mask) * each, 8)
            for sheet in range(sheets):
                line = (n * sheets + sheet) * each
                turned[sheet, pl.ds(at, each), :] = value[line:line + each]
    times = sheets // 2
    for sheet in range(sheets):
        target = volt_re if sheet < times else volt_im
        facing = turned[sheet].T
        for g in range(chans // 8):
            at = (g * times + sheet % times) * 8
            target[at:at + 8, :] = facing[g * 8:g * 8 + 8]
    span = 8 * times

    def prepare(q, x_out):
        pr = phase_re[pl.ds(q, 1), :]
        pi = phase_im[pl.ds(q, 1), :]
        for g in range(chans // 8):
            vr = volt_re[g * span:(g + 1) * span, :]
            vi = volt_im[g * span:(g + 1) * span, :]
            xr = (vr * pr - vi * pi).astype(jnp.bfloat16)
            xi = (vr * pi + vi * pr).astype(jnp.bfloat16)
            real = slice(2 * g * span, (2 * g + 1) * span)
            imag = slice((2 * g + 1) * span, (2 * g + 2) * span)
            x_out[real, :stations] = xr
            x_out[real, stations:] = -xi
            x_out[imag, :stations] = xi
            x_out[imag, stations:] = xr

    top = chans // 8
    step_of = top + (2.0 * whole_of((8, TILE), 0).astype(jnp.float32) + 1.0 - chans) * 0.0625

    def collect(q, tile, field):
        s0, s1, s2 = None, None, None
        for g in range(top):
            for t in range(2 * times):
                line = (g * 2 * times + t) * 8
                part = field[line:line + 8, :]
                total = part * part if t == 0 else total + part * part
            s0 = total if g == 0 else s0 + total
            s1 = s0 if g == 0 else s1 + s0
            s2 = s1 if g == 0 else s2 + s1
        first = step_of * s0 - s1
        second = step_of * (step_of * s0 - 2.0 * s1) + (2.0 * s2 - s1)
        for k, value in enumerate((s0, first, second)):
            sums[k, pl.ds(q, 1), tile * TILE:(tile + 1) * TILE] = norm[k] * jnp.sum(value, axis=0, keepdims=True)

    tiles = lanes // TILE
    xs = (x_a, x_b)
    prepare(0, x_a)

    def chunk(q, turn, response, index):
        for n in range(tiles):
            field = jnp.dot(
                xs[turn][...], response[index, :, n * TILE:(n + 1) * TILE], preferred_element_type=jnp.float32
            )
            if n == 0:
                prepare(jnp.minimum(q + 1, steps - 1), xs[1 - turn])
            collect(q, n, field)

    base, turn = 0, 0
    for response in responses:
        here = response.shape[0]

        def two(i, carry):
            for j in range(2):
                chunk(base + 2 * i + j, (turn + j) % 2, response, 2 * i + j)
            return carry

        lax.fori_loop(0, here // 2, two, 0)
        if here % 2:
            chunk(base + here - 1, turn, response, here - 1)
        base, turn = base + here, (turn + here) % 2
    for k in range(3):
        for p in range(STEP):
            for j in range(strips.shape[0]):
                at = p * width + j * 128
                strips[j, pl.ds(p, steps, stride=STEP), :] = sums[k, :, at:at + 128]
        for j in range(strips.shape[0]):
            left = min(128, width - j * 128)
            out[k, :, j * 128:j * 128 + left] = strips[j, :, :left]


def local(cells, voltages, kernel_table, station_rows, station_cols, kernel_offset):
    times, chans = voltages.shape[1], voltages.shape[2]
    stations = station_rows.shape[0]
    variants, taps = kernel_table.shape[0], kernel_table.shape[1]
    count = lax.axis_size("chan")
    height = cells // count
    width = cells // lax.axis_size("row")
    here = lax.axis_index("chan")
    steps = height // STEP
    lanes = STEP * width
    planes = times * chans
    place = jnp.stack([here * 0, here * height, lax.axis_index("row") * width]).astype(jnp.int32)
    vmem = pl.BlockSpec(memory_space=pltpu.VMEM)
    smem = pl.BlockSpec(memory_space=pltpu.SMEM)
    f32, bf16 = jnp.float32, jnp.bfloat16
    mib = 1024 * 1024

    hbm = pl.BlockSpec(memory_space=pltpu.HBM)
    joined = ((station_rows * cells + station_cols) * variants + kernel_offset).reshape(1, stations)
    own = voltages.transpose(0, 1, 3, 2).reshape(2 * times * voltages.shape[3], chans)
    make_tables = lambda: pl.pallas_call(
        lambda *refs: table_kernel(cells, width, *refs),
        out_shape=[
            jax.ShapeDtypeStruct((stations, lanes), f32),
            jax.ShapeDtypeStruct((stations, lanes), f32),
            jax.ShapeDtypeStruct((stations, 128), jnp.int32),
            jax.ShapeDtypeStruct((steps, 8, lanes), f32),
            jax.ShapeDtypeStruct((steps, 8, lanes), f32),
            jax.ShapeDtypeStruct((steps, stations), f32),
            jax.ShapeDtypeStruct((steps, stations), f32),
        ],
        in_specs=[smem] + [hbm] * 2,
        out_specs=[vmem] * 7,
        scratch_shapes=[
            pltpu.VMEM((1, stations), jnp.int32),
            pltpu.VMEM((variants * taps, taps), bf16),
            pltpu.SemaphoreType.DMA((2,)),
        ],
        compiler_params=pltpu.CompilerParams(vmem_limit_bytes=16 * mib),
        cost_estimate=pl.CostEstimate(flops=100 * stations * lanes, bytes_accessed=16 * stations * lanes, transcendentals=0),
    )(place, joined, kernel_table.reshape(variants * taps, taps))

    gathered = lax.all_gather(own, "chan", axis=0, tiled=True)
    *tables, phase_re, phase_im = make_tables()
    responses = [pl.pallas_call(
        lambda *refs: response_kernel(0, *refs),
        out_shape=jax.ShapeDtypeStruct((steps, 2 * stations, lanes), bf16),
        in_specs=[vmem] * 5,
        out_specs=vmem,
        compiler_params=pltpu.CompilerParams(vmem_limit_bytes=16 * mib),
        cost_estimate=pl.CostEstimate(
            flops=16 * steps * stations * lanes, bytes_accessed=4 * steps * stations * lanes, transcendentals=0
        ),
    )(*tables)]
    blocks, masks = [gathered], [tuple(range(count))]

    x = (2.0 * np.arange(chans) + 1.0 - chans) / chans
    norm = [
        float(1.0 / np.sqrt(np.sum(x ** (2 * k))) / (times * stations * taps * taps) * (16.0 / chans) ** k)
        for k in range(3)
    ]
    groups = (len(blocks), len(responses))
    return pl.pallas_call(
        lambda *refs: image_kernel(chans, width, norm, masks, groups, *refs),
        out_shape=jax.ShapeDtypeStruct((3, height, width), f32),
        in_specs=[smem] + [vmem] * (2 + sum(groups)),
        out_specs=vmem,
        scratch_shapes=[
            pltpu.VMEM((2 * times, stations, chans), f32),
            pltpu.VMEM((planes, stations), f32),
            pltpu.VMEM((planes, stations), f32),
            pltpu.VMEM((2 * planes, 2 * stations), bf16),
            pltpu.VMEM((2 * planes, 2 * stations), bf16),
            pltpu.VMEM((3, steps, lanes + 128), f32),
            pltpu.VMEM((-(-width // 128), height, 128), f32),
        ],
        compiler_params=pltpu.CompilerParams(vmem_limit_bytes=32 * mib),
        cost_estimate=pl.CostEstimate(
            flops=8 * steps * planes * stations * lanes, bytes_accessed=4 * steps * stations * lanes, transcendentals=0
        ),
    )(place, phase_re, phase_im, *blocks, *responses)


def solution(mesh):
    cells = 768
    placed = (P(None, None, None, "chan"), P(), P(), P(), P())
    return jax.shard_map(
        lambda *args: local(cells, *args), mesh=mesh, in_specs=placed, out_specs=P(None, "chan", "row"), check_vma=False
    )
```

```python
import jax
import jax.numpy as jnp
import numpy as np
from jax import lax
from jax.experimental import pallas as pl
from jax.experimental.pallas import tpu as pltpu
from jax.sharding import PartitionSpec as P

TILE = 512
ROWS = 256
STEP = 8


def wave_fit(terms=7):
    nodes = 0.125 + 0.125 * np.cos(np.pi * (np.arange(200) + 0.5) / 200)
    root = np.sqrt(nodes)
    fit = np.polynomial.polynomial.polyfit
    cosine = fit(nodes, np.cos(2 * np.pi * root), terms - 1)
    sine = fit(nodes, np.sin(2 * np.pi * root) / root, terms - 1)
    return [float(c) for c in cosine], [float(c) for c in sine]


COS_FIT, SIN_FIT = wave_fit()


def horner(coefs, x):
    value = jnp.full_like(x, coefs[-1])
    for c in coefs[-2::-1]:
        value = value * x + c
    return value


def wave(product, cells):
    turns = product * (1.0 / cells)
    part = (product - cells * jnp.round(turns)) * (1.0 / cells)
    square = part * part
    return horner(COS_FIT, square), -part * horner(SIN_FIT, square)


def whole_of(shape, axis):
    return lax.broadcasted_iota(jnp.int32, shape, axis)


def split(value):
    high = value.astype(jnp.bfloat16)
    return high, (value - high.astype(jnp.float32)).astype(jnp.bfloat16)


def station_column(values, stations):
    return jnp.broadcast_to(values, (128, stations)).T


def table_kernel(
    cells, taps, variants, width, place, held_in, joined_in,
    base_re, base_im, pick, spread_re, spread_im, phase_re, phase_im, held, joined, right_re, right_im, arrived
):
    copies = [
        pltpu.make_async_copy(source, target, arrived.at[n])
        for n, (source, target) in enumerate((
            (joined_in, joined), (held_in, held),
        ))
    ]
    for copy in copies:
        copy.start()
    for copy in copies:
        copy.wait()
    stations = base_re.shape[0]
    steps, lanes = spread_re.shape[0], spread_re.shape[2]
    first_row = place[1].astype(jnp.float32)
    first_col = place[2].astype(jnp.float32)
    kinds = variants * taps
    kernels = joined[:kinds, :taps].astype(jnp.bfloat16)
    code = jnp.concatenate([joined[kinds + n:kinds + n + 1, :] for n in range(stations // 128)], axis=1)
    rows = jnp.floor((code + 0.5) * (1.0 / (cells * variants)))
    code = code - rows * float(cells * variants)
    cols = jnp.floor((code + 0.5) * (1.0 / variants))
    pick[...] = station_column(code - cols * float(variants), stations).astype(jnp.int32)
    row_of = station_column(rows, stations)
    col_of = station_column(cols, stations)
    start = first_row + float(STEP) * whole_of((steps, stations), 0).astype(jnp.float32)
    phase_re[...], phase_im[...] = wave(start * rows, cells)

    def down_across(shape, start):
        lane = whole_of(shape, 1) + start
        down = jnp.zeros(shape, jnp.float32)
        for p in range(1, STEP):
            down = jnp.where(lane >= p * width, float(p), down)
        return down, lane.astype(jnp.float32) - down * width + first_col

    half = lanes // 2
    leap_re, leap_im = wave(row_of * float(STEP // 2), cells)
    for tile in range(half // 128):
        at = slice(tile * 128, (tile + 1) * 128)
        later = slice(half + tile * 128, half + (tile + 1) * 128)
        down, across = down_across((stations, 128), tile * 128)
        real, imag = wave(row_of * down + col_of * across, cells)
        base_re[:, at], base_im[:, at] = real, imag
        base_re[:, later] = real * leap_re - imag * leap_im
        base_im[:, later] = real * leap_im + imag * leap_re

    down, across = down_across((taps, lanes), 0)
    tap = whole_of((taps, lanes), 0).astype(jnp.float32)

    def over_columns(value):
        high, low = split(value)
        return jnp.dot(kernels, high, preferred_element_type=jnp.float32) + jnp.dot(
            kernels, low, preferred_element_type=jnp.float32
        )

    half_re, half_im = [over_columns(value) for value in wave(tap * across, cells)]
    turn_re, turn_im = wave(tap * down, cells)
    stride = 128
    tall = -(-steps * 8 // 16) * 16
    shape = (tall, stride)
    row, lane = whole_of(shape, 0), whole_of(shape, 1)
    start = first_row + float(STEP) * (row >> 3).astype(jnp.float32)
    left_re, left_im = wave(start * (lane & (taps - 1)).astype(jnp.float32), cells)
    value = jnp.where((lane & taps) == 0, left_re, -left_im)
    high, low = split(value)
    second = (lane >= 2 * taps) & (lane < 4 * taps)
    value = jnp.where(second, low.astype(jnp.float32), high.astype(jnp.float32))
    left = jnp.concatenate(
        [jnp.where(((row & 7) == o) & (lane < 6 * taps), value, 0.0) for o in range(variants)], axis=1
    ).astype(jnp.bfloat16)
    rest = jnp.zeros((stride - 6 * taps, lanes), jnp.bfloat16)
    for o in range(variants):
        rows_o = slice(o * taps, (o + 1) * taps)
        real = turn_re * half_re[rows_o] - turn_im * half_im[rows_o]
        imag = turn_re * half_im[rows_o] + turn_im * half_re[rows_o]
        real_high, real_low = split(real)
        imag_high, imag_low = split(imag)
        for target, parts in (
            (right_re, (real_high, imag_high, real_high, imag_high, real_low, imag_low)),
            (right_im, (imag_high, -real_high, imag_high, -real_high, imag_low, -real_low)),
        ):
            for n, part in enumerate(parts):
                target[o * stride + n * taps:o * stride + (n + 1) * taps, :] = part
            target[o * stride + 6 * taps:(o + 1) * stride, :] = rest
    for target, right in ((spread_re, right_re), (spread_im, right_im)):
        spectra = jnp.dot(left, right[...], preferred_element_type=jnp.float32)
        for q in range(steps):
            target[q] = spectra[q * 8:q * 8 + 8]


def response_kernel(first, held, base_re, base_im, pick, spread_re, spread_im, response, kept):
    kept[...] = held[...]
    parts, stations, lanes = response.shape[0], base_re.shape[0], base_re.shape[1]
    joint = 2 if parts % 2 == 0 else 1

    def some(i, carry):
        for tile in range(lanes // 128):
            at = slice(tile * 128, (tile + 1) * 128)
            tables = [
                (spread_re[first + joint * i + j, :, at], spread_im[first + joint * i + j, :, at]) for j in range(joint)
            ]
            for group in range(stations // 16):
                made = [([], []) for j in range(joint)]
                for half in range(2):
                    sub = slice(group * 16 + half * 8, group * 16 + half * 8 + 8)
                    index = pick[sub, :]
                    br = base_re[sub, at]
                    bi = base_im[sub, at]
                    for j in range(joint):
                        sr = jnp.take_along_axis(tables[j][0], index, axis=0)
                        si = jnp.take_along_axis(tables[j][1], index, axis=0)
                        made[j][0].append(br * sr - bi * si)
                        made[j][1].append(br * si + bi * sr)
                pair = slice(group * 16, group * 16 + 16)
                low = slice(stations + group * 16, stations + group * 16 + 16)
                for j in range(joint):
                    response[joint * i + j, pair, at] = jnp.concatenate(made[j][0], axis=0).astype(jnp.bfloat16)
                    response[joint * i + j, low, at] = jnp.concatenate(made[j][1], axis=0).astype(jnp.bfloat16)
        return carry

    lax.fori_loop(0, parts // joint, some, 0)


def image_kernel(
    chans, width, norm, masks, groups, place, phase_re, phase_im, *refs
):
    blocks, responses = refs[:groups[0]], refs[groups[0]:sum(groups)]
    out, turned, volt_re, volt_im, x_a, x_b, sums, strips = refs[sum(groups):]
    planes, stations = volt_re.shape
    steps, lanes = phase_re.shape[0], responses[0].shape[2]
    sheets = turned.shape[0]
    each = stations // len(sum(masks, ()))

    for block, held in zip(blocks, masks):
        value = block[...].astype(jnp.float32)
        for n, mask in enumerate(held):
            at = pl.multiple_of((place[0] ^ mask) * each, 8)
            for sheet in range(sheets):
                line = (n * sheets + sheet) * each
                turned[sheet, pl.ds(at, each), :] = value[line:line + each]
    times = sheets // 2
    for sheet in range(sheets):
        target = volt_re if sheet < times else volt_im
        facing = turned[sheet].T
        for g in range(chans // 8):
            at = (g * times + sheet % times) * 8
            target[at:at + 8, :] = facing[g * 8:g * 8 + 8]
    span = 8 * times

    def prepare(q, x_out):
        pr = phase_re[pl.ds(q, 1), :]
        pi = phase_im[pl.ds(q, 1), :]
        for g in range(chans // 8):
            vr = volt_re[g * span:(g + 1) * span, :]
            vi = volt_im[g * span:(g + 1) * span, :]
            xr = (vr * pr - vi * pi).astype(jnp.bfloat16)
            xi = (vr * pi + vi * pr).astype(jnp.bfloat16)
            real = slice(2 * g * span, (2 * g + 1) * span)
            imag = slice((2 * g + 1) * span, (2 * g + 2) * span)
            x_out[real, :stations] = xr
            x_out[real, stations:] = -xi
            x_out[imag, :stations] = xi
            x_out[imag, stations:] = xr

    top = chans // 8
    step_of = top + (2.0 * whole_of((8, TILE), 0).astype(jnp.float32) + 1.0 - chans) * 0.0625

    def gather_sums(field, totals):
        s0, s1, s2 = totals
        for g in range(field.shape[0] // (2 * span)):
            for t in range(2 * times):
                line = (g * 2 * times + t) * 8
                part = field[line:line + 8, :]
                total = part * part if t == 0 else total + part * part
            s0 = s0 + total
            s1 = s1 + s0
            s2 = s2 + s1
        return s0, s1, s2

    def collect(q, tile, totals):
        s0, s1, s2 = totals
        first = step_of * s0 - s1
        second = step_of * (step_of * s0 - 2.0 * s1) + (2.0 * s2 - s1)
        for k, value in enumerate((s0, first, second)):
            sums[k, pl.ds(q, 1), tile * TILE:(tile + 1) * TILE] = norm[k] * jnp.sum(value, axis=0, keepdims=True)

    tiles = lanes // TILE
    xs = (x_a, x_b)
    prepare(0, x_a)

    def chunk(q, turn, response, index):
        for n in range(tiles):
            totals = (jnp.zeros((8, TILE), jnp.float32),) * 3
            for m in range(planes * 2 // ROWS):
                field = jnp.dot(
                    xs[turn][m * ROWS:(m + 1) * ROWS, :], response[index, :, n * TILE:(n + 1) * TILE],
                    preferred_element_type=jnp.float32,
                )
                if n == 0 and m == 0:
                    prepare(jnp.minimum(q + 1, steps - 1), xs[1 - turn])
                totals = gather_sums(field, totals)
            collect(q, n, totals)

    base, turn = 0, 0
    for response in responses:
        here = response.shape[0]

        def two(i, carry):
            for j in range(2):
                chunk(base + 2 * i + j, (turn + j) % 2, response, 2 * i + j)
            return carry

        lax.fori_loop(0, here // 2, two, 0)
        if here % 2:
            chunk(base + here - 1, turn, response, here - 1)
        base, turn = base + here, (turn + here) % 2
    for k in range(3):
        for p in range(STEP):
            for j in range(strips.shape[0]):
                at = p * width + j * 128
                strips[j, pl.ds(p, steps, stride=STEP), :] = sums[k, :, at:at + 128]
        for j in range(strips.shape[0]):
            left = min(128, width - j * 128)
            out[k, :, j * 128:j * 128 + left] = strips[j, :, :left]


def local(cells, voltages, kernel_table, station_rows, station_cols, kernel_offset):
    times, chans = voltages.shape[1], voltages.shape[2]
    stations = station_rows.shape[0]
    variants, taps = kernel_table.shape[0], kernel_table.shape[1]
    count = lax.axis_size("chan")
    height = cells // count
    width = cells // lax.axis_size("row")
    here = lax.axis_index("chan")
    steps = height // STEP
    lanes = STEP * width
    planes = times * chans
    place = jnp.stack([here, here * height, lax.axis_index("row") * width]).astype(jnp.int32)
    vmem = pl.BlockSpec(memory_space=pltpu.VMEM)
    smem = pl.BlockSpec(memory_space=pltpu.SMEM)
    f32, bf16 = jnp.float32, jnp.bfloat16
    mib = 1024 * 1024

    bits = []
    while (1 << len(bits)) < count:
        bits.append(count >> (len(bits) + 1))
    hbm = pl.BlockSpec(memory_space=pltpu.HBM)
    code = ((station_rows * cells + station_cols) * variants + kernel_offset).astype(f32).reshape(stations // 128, 128)
    shapes = kernel_table.reshape(variants * taps, taps).astype(f32)
    joined = jnp.concatenate([jnp.pad(shapes, ((0, 0), (0, 128 - taps))), code])
    own = voltages.transpose(0, 1, 3, 2).reshape(2 * times * voltages.shape[3], chans)
    make_tables = lambda: pl.pallas_call(
        lambda *refs: table_kernel(cells, taps, variants, width, *refs),
        out_shape=[
            jax.ShapeDtypeStruct((stations, lanes), f32),
            jax.ShapeDtypeStruct((stations, lanes), f32),
            jax.ShapeDtypeStruct((stations, 128), jnp.int32),
            jax.ShapeDtypeStruct((steps, 8, lanes), f32),
            jax.ShapeDtypeStruct((steps, 8, lanes), f32),
            jax.ShapeDtypeStruct((steps, stations), f32),
            jax.ShapeDtypeStruct((steps, stations), f32),
            jax.ShapeDtypeStruct(own.shape, bf16),
        ],
        in_specs=[smem] + [hbm] * 2,
        out_specs=[vmem] * 8,
        scratch_shapes=[
            pltpu.VMEM(joined.shape, f32),
            pltpu.VMEM((variants * 128, lanes), bf16),
            pltpu.VMEM((variants * 128, lanes), bf16),
            pltpu.SemaphoreType.DMA((2,)),
        ],
        compiler_params=pltpu.CompilerParams(vmem_limit_bytes=16 * mib),
        cost_estimate=pl.CostEstimate(flops=100 * stations * lanes, bytes_accessed=16 * stations * lanes, transcendentals=0),
    )(place, own, joined)

    ahead = steps // 2
    shares = [(0, steps - ahead), (steps - ahead, ahead)]
    held, reach, responses = own, (0,), []
    for cut, bit in enumerate(bits):
        came = lax.ppermute(held, "chan", [(j, j ^ bit) for j in range(count)])
        if cut == 0:
            *tables, phase_re, phase_im, held = make_tables()
        elif cut <= len(shares):
            first, part = shares[cut - 1]
            response, held = pl.pallas_call(
                lambda *refs, first=first: response_kernel(first, *refs),
                out_shape=[
                    jax.ShapeDtypeStruct((part, 2 * stations, lanes), bf16),
                    jax.ShapeDtypeStruct(held.shape, bf16),
                ],
                in_specs=[vmem] * 6,
                out_specs=[vmem] * 2,
                compiler_params=pltpu.CompilerParams(vmem_limit_bytes=16 * mib),
                cost_estimate=pl.CostEstimate(
                    flops=16 * part * stations * lanes, bytes_accessed=4 * part * stations * lanes, transcendentals=0
                ),
            )(held, *tables)
            responses.append(response)
        masks = [reach, tuple(m ^ bit for m in reach)]
        reach = sum(masks, ())
        blocks = [held, came]
        held = jnp.concatenate(blocks)

    x = (2.0 * np.arange(chans) + 1.0 - chans) / chans
    norm = [
        float(1.0 / np.sqrt(np.sum(x ** (2 * k))) / (times * stations * taps * taps) * (16.0 / chans) ** k)
        for k in range(3)
    ]
    groups = (len(blocks), len(responses))
    return pl.pallas_call(
        lambda *refs: image_kernel(chans, width, norm, masks, groups, *refs),
        out_shape=jax.ShapeDtypeStruct((3, height, width), f32),
        in_specs=[smem] + [vmem] * (2 + sum(groups)),
        out_specs=vmem,
        scratch_shapes=[
            pltpu.VMEM((2 * times, stations, chans), f32),
            pltpu.VMEM((planes, stations), f32),
            pltpu.VMEM((planes, stations), f32),
            pltpu.VMEM((2 * planes, 2 * stations), bf16),
            pltpu.VMEM((2 * planes, 2 * stations), bf16),
            pltpu.VMEM((3, steps, lanes + 128), f32),
            pltpu.VMEM((-(-width // 128), height, 128), f32),
        ],
        compiler_params=pltpu.CompilerParams(vmem_limit_bytes=32 * mib),
        cost_estimate=pl.CostEstimate(
            flops=8 * steps * planes * stations * lanes, bytes_accessed=4 * steps * stations * lanes, transcendentals=0
        ),
    )(place, phase_re, phase_im, *blocks, *responses)


def solution(mesh):
    cells = 768
    placed = (P(None, None, None, "chan"), P(), P(), P(), P())
    return jax.shard_map(
        lambda *args: local(cells, *args), mesh=mesh, in_specs=placed, out_specs=P(None, "chan", "row"), check_vma=False
    )
```

```python
import jax
import jax.numpy as jnp
import numpy as np
from jax import lax
from jax.experimental import pallas as pl
from jax.experimental.pallas import tpu as pltpu
from jax.sharding import PartitionSpec as P

TILE = 512
ROWS = 512
STEP = 8


def wave_fit(terms=7):
    nodes = 0.125 + 0.125 * np.cos(np.pi * (np.arange(200) + 0.5) / 200)
    root = np.sqrt(nodes)
    fit = np.polynomial.polynomial.polyfit
    cosine = fit(nodes, np.cos(2 * np.pi * root), terms - 1)
    sine = fit(nodes, np.sin(2 * np.pi * root) / root, terms - 1)
    return [float(c) for c in cosine], [float(c) for c in sine]


COS_FIT, SIN_FIT = wave_fit()


def horner(coefs, x):
    value = jnp.full_like(x, coefs[-1])
    for c in coefs[-2::-1]:
        value = value * x + c
    return value


def wave(product, cells):
    turns = product * (1.0 / cells)
    part = (product - cells * jnp.round(turns)) * (1.0 / cells)
    square = part * part
    return horner(COS_FIT, square), -part * horner(SIN_FIT, square)


def whole_of(shape, axis):
    return lax.broadcasted_iota(jnp.int32, shape, axis)


def split(value):
    high = value.astype(jnp.bfloat16)
    return high, (value - high.astype(jnp.float32)).astype(jnp.bfloat16)


def station_column(values, stations):
    return jnp.broadcast_to(values, (128, stations)).T


def down_across(shape, start, width, first_col):
    lane = whole_of(shape, 1) + start
    down = jnp.zeros(shape, jnp.float32)
    for p in range(1, STEP):
        down = jnp.where(lane >= p * width, float(p), down)
    return down, lane.astype(jnp.float32) - down * width + first_col


def table_kernel(
    cells, variants, width, place, held_in, joined_in,
    base_re, base_im, pick, phase_re, phase_im, held, joined, arrived
):
    copies = [
        pltpu.make_async_copy(source, target, arrived.at[n])
        for n, (source, target) in enumerate(((joined_in, joined), (held_in, held)))
    ]
    for copy in copies:
        copy.start()
    for copy in copies:
        copy.wait()
    stations, lanes = base_re.shape
    steps = phase_re.shape[0]
    first_row = place[1].astype(jnp.float32)
    first_col = place[2].astype(jnp.float32)
    code = jnp.concatenate([joined[n:n + 1, :] for n in range(stations // 128)], axis=1)
    rows = jnp.floor((code + 0.5) * (1.0 / (cells * variants)))
    code = code - rows * float(cells * variants)
    cols = jnp.floor((code + 0.5) * (1.0 / variants))
    pick[...] = station_column(code - cols * float(variants), stations).astype(jnp.int32)
    row_of = station_column(rows, stations)
    col_of = station_column(cols, stations)
    start = first_row + float(STEP) * whole_of((steps, stations), 0).astype(jnp.float32)
    phase_re[...], phase_im[...] = wave(start * rows, cells)
    half = lanes // 2
    leap_re, leap_im = wave(row_of * float(STEP // 2), cells)
    for tile in range(half // 128):
        at = slice(tile * 128, (tile + 1) * 128)
        later = slice(half + tile * 128, half + (tile + 1) * 128)
        down, across = down_across((stations, 128), tile * 128, width, first_col)
        real, imag = wave(row_of * down + col_of * across, cells)
        base_re[:, at], base_im[:, at] = real, imag
        base_re[:, later] = real * leap_re - imag * leap_im
        base_im[:, later] = real * leap_im + imag * leap_re


def make_spectra(cells, taps, variants, width, place, table, spread_re, spread_im, right_re, right_im):
    steps, lanes = spread_re.shape[0], spread_re.shape[2]
    kernels = table[...]
    first_row = place[1].astype(jnp.float32)
    down, across = down_across((taps, lanes), 0, width, place[2].astype(jnp.float32))
    tap = whole_of((taps, lanes), 0).astype(jnp.float32)

    def over_columns(value):
        high, low = split(value)
        return jnp.dot(kernels, high, preferred_element_type=jnp.float32) + jnp.dot(
            kernels, low, preferred_element_type=jnp.float32
        )

    half_re, half_im = [over_columns(value) for value in wave(tap * across, cells)]
    turn_re, turn_im = wave(tap * down, cells)
    stride = 128
    tall = -(-steps * 8 // 16) * 16
    shape = (tall, stride)
    row, lane = whole_of(shape, 0), whole_of(shape, 1)
    start = first_row + float(STEP) * (row >> 3).astype(jnp.float32)
    left_re, left_im = wave(start * (lane & (taps - 1)).astype(jnp.float32), cells)
    value = jnp.where((lane & taps) == 0, left_re, -left_im)
    high, low = split(value)
    second = (lane >= 2 * taps) & (lane < 4 * taps)
    value = jnp.where(second, low.astype(jnp.float32), high.astype(jnp.float32))
    left = jnp.concatenate(
        [jnp.where(((row & 7) == o) & (lane < 6 * taps), value, 0.0) for o in range(variants)], axis=1
    ).astype(jnp.bfloat16)
    rest = jnp.zeros((stride - 6 * taps, lanes), jnp.bfloat16)
    for o in range(variants):
        rows_o = slice(o * taps, (o + 1) * taps)
        real = turn_re * half_re[rows_o] - turn_im * half_im[rows_o]
        imag = turn_re * half_im[rows_o] + turn_im * half_re[rows_o]
        real_high, real_low = split(real)
        imag_high, imag_low = split(imag)
        for target, parts in (
            (right_re, (real_high, imag_high, real_high, imag_high, real_low, imag_low)),
            (right_im, (imag_high, -real_high, imag_high, -real_high, imag_low, -real_low)),
        ):
            for n, part in enumerate(parts):
                target[o * stride + n * taps:o * stride + (n + 1) * taps, :] = part
            target[o * stride + 6 * taps:(o + 1) * stride, :] = rest
    for target, right in ((spread_re, right_re), (spread_im, right_im)):
        spectra = jnp.dot(left, right[...], preferred_element_type=jnp.float32)
        for q in range(steps):
            target[q] = spectra[q * 8:q * 8 + 8]


def respond(first, base_re, base_im, pick, spread_re, spread_im, response, variants):
    parts, stations, lanes = response.shape[0], base_re.shape[0], base_re.shape[1]
    joint = 2 if parts % 2 == 0 else 1

    def some(i, carry):
        for tile in range(lanes // 128):
            at = slice(tile * 128, (tile + 1) * 128)
            here = [first + joint * i + j for j in range(joint)]
            tables = [spread_re[q, :, at] for q in here]
            choices = [
                [jnp.broadcast_to(spread_im[q, o:o + 1, at], (8, 128)) for o in range(variants)] for q in here
            ]
            for group in range(stations // 16):
                made = [([], []) for j in range(joint)]
                for half in range(2):
                    sub = slice(group * 16 + half * 8, group * 16 + half * 8 + 8)
                    index = pick[sub, :]
                    chosen = [index == o for o in range(1, variants)]
                    br = base_re[sub, at]
                    bi = base_im[sub, at]
                    for j in range(joint):
                        sr = jnp.take_along_axis(tables[j], index, axis=0)
                        si = choices[j][0]
                        for o in range(1, variants):
                            si = jnp.where(chosen[o - 1], choices[j][o], si)
                        made[j][0].append(br * sr - bi * si)
                        made[j][1].append(br * si + bi * sr)
                pair = slice(group * 16, group * 16 + 16)
                low = slice(stations + group * 16, stations + group * 16 + 16)
                for j in range(joint):
                    response[joint * i + j, pair, at] = jnp.concatenate(made[j][0], axis=0).astype(jnp.bfloat16)
                    response[joint * i + j, low, at] = jnp.concatenate(made[j][1], axis=0).astype(jnp.bfloat16)
        return carry

    lax.fori_loop(0, parts // joint, some, 0)


def first_kernel(
    cells, taps, variants, width, place, held, table, base_re, base_im, pick,
    response, kept, spread_re, spread_im, right_re, right_im
):
    kept[...] = held[...]
    make_spectra(cells, taps, variants, width, place, table, spread_re, spread_im, right_re, right_im)
    respond(0, base_re, base_im, pick, spread_re, spread_im, response, variants)


def second_kernel(first, variants, held, base_re, base_im, pick, spread_re, spread_im, response, kept):
    kept[...] = held[...]
    respond(first, base_re, base_im, pick, spread_re, spread_im, response, variants)


def image_kernel(
    chans, width, norm, masks, groups, place, phase_re, phase_im, *refs
):
    blocks, responses = refs[:groups[0]], refs[groups[0]:sum(groups)]
    out, turned, volt_re, volt_im, x_a, x_b, sums, strips = refs[sum(groups):]
    planes, stations = volt_re.shape
    steps, lanes = phase_re.shape[0], responses[0].shape[2]
    sheets = turned.shape[0]
    each = stations // len(sum(masks, ()))

    for block, held in zip(blocks, masks):
        value = block[...].astype(jnp.float32)
        for n, mask in enumerate(held):
            at = pl.multiple_of((place[0] ^ mask) * each, 8)
            for sheet in range(sheets):
                line = (n * sheets + sheet) * each
                turned[sheet, pl.ds(at, each), :] = value[line:line + each]
    times = sheets // 2
    for sheet in range(sheets):
        target = volt_re if sheet < times else volt_im
        facing = turned[sheet].T
        for g in range(chans // 8):
            at = (g * times + sheet % times) * 8
            target[at:at + 8, :] = facing[g * 8:g * 8 + 8]
    span = 8 * times

    def prepare(q, x_out):
        pr = phase_re[pl.ds(q, 1), :]
        pi = phase_im[pl.ds(q, 1), :]
        for g in range(chans // 8):
            vr = volt_re[g * span:(g + 1) * span, :]
            vi = volt_im[g * span:(g + 1) * span, :]
            xr = (vr * pr - vi * pi).astype(jnp.bfloat16)
            xi = (vr * pi + vi * pr).astype(jnp.bfloat16)
            real = slice(2 * g * span, (2 * g + 1) * span)
            imag = slice((2 * g + 1) * span, (2 * g + 2) * span)
            x_out[real, :stations] = xr
            x_out[real, stations:] = -xi
            x_out[imag, :stations] = xi
            x_out[imag, stations:] = xr

    top = chans // 8
    step_of = top + (2.0 * whole_of((8, TILE), 0).astype(jnp.float32) + 1.0 - chans) * 0.0625

    def gather_sums(field, totals):
        s0, s1, s2 = totals
        for g in range(field.shape[0] // (2 * span)):
            for t in range(2 * times):
                line = (g * 2 * times + t) * 8
                part = field[line:line + 8, :]
                total = part * part if t == 0 else total + part * part
            s0 = s0 + total
            s1 = s1 + s0
            s2 = s2 + s1
        return s0, s1, s2

    def collect(q, tile, totals):
        s0, s1, s2 = totals
        first = step_of * s0 - s1
        second = step_of * (step_of * s0 - 2.0 * s1) + (2.0 * s2 - s1)
        for k, value in enumerate((s0, first, second)):
            sums[k, pl.ds(q, 1), tile * TILE:(tile + 1) * TILE] = norm[k] * jnp.sum(value, axis=0, keepdims=True)

    tiles = lanes // TILE
    xs = (x_a, x_b)
    prepare(0, x_a)

    def chunk(q, turn, response, index):
        for n in range(tiles):
            totals = (jnp.zeros((8, TILE), jnp.float32),) * 3
            for m in range(planes * 2 // ROWS):
                field = jnp.dot(
                    xs[turn][m * ROWS:(m + 1) * ROWS, :], response[index, :, n * TILE:(n + 1) * TILE],
                    preferred_element_type=jnp.float32,
                )
                if n == 0 and m == 0:
                    prepare(jnp.minimum(q + 1, steps - 1), xs[1 - turn])
                totals = gather_sums(field, totals)
            collect(q, n, totals)

    base, turn = 0, 0
    for response in responses:
        here = response.shape[0]

        def two(i, carry):
            for j in range(2):
                chunk(base + 2 * i + j, (turn + j) % 2, response, 2 * i + j)
            return carry

        lax.fori_loop(0, here // 2, two, 0)
        if here % 2:
            chunk(base + here - 1, turn, response, here - 1)
        base, turn = base + here, (turn + here) % 2
    for k in range(3):
        for p in range(STEP):
            for j in range(strips.shape[0]):
                at = p * width + j * 128
                strips[j, pl.ds(p, steps, stride=STEP), :] = sums[k, :, at:at + 128]
        for j in range(strips.shape[0]):
            left = min(128, width - j * 128)
            out[k, :, j * 128:j * 128 + left] = strips[j, :, :left]


def local(cells, voltages, kernel_table, station_rows, station_cols, kernel_offset):
    times, chans = voltages.shape[1], voltages.shape[2]
    stations = station_rows.shape[0]
    variants, taps = kernel_table.shape[0], kernel_table.shape[1]
    count = lax.axis_size("chan")
    height = cells // count
    width = cells // lax.axis_size("row")
    here = lax.axis_index("chan")
    steps = height // STEP
    lanes = STEP * width
    planes = times * chans
    place = jnp.stack([here, here * height, lax.axis_index("row") * width]).astype(jnp.int32)
    vmem = pl.BlockSpec(memory_space=pltpu.VMEM)
    smem = pl.BlockSpec(memory_space=pltpu.SMEM)
    f32, bf16 = jnp.float32, jnp.bfloat16
    mib = 1024 * 1024

    bits = []
    while (1 << len(bits)) < count:
        bits.append(count >> (len(bits) + 1))
    hbm = pl.BlockSpec(memory_space=pltpu.HBM)
    code = ((station_rows * cells + station_cols) * variants + kernel_offset).astype(f32).reshape(stations // 128, 128)
    shapes = kernel_table.reshape(variants * taps, taps)
    own = voltages.transpose(0, 1, 3, 2).reshape(2 * times * voltages.shape[3], chans)
    make_tables = lambda: pl.pallas_call(
        lambda *refs: table_kernel(cells, variants, width, *refs),
        out_shape=[
            jax.ShapeDtypeStruct((stations, lanes), f32),
            jax.ShapeDtypeStruct((stations, lanes), f32),
            jax.ShapeDtypeStruct((stations, 128), jnp.int32),
            jax.ShapeDtypeStruct((steps, stations), f32),
            jax.ShapeDtypeStruct((steps, stations), f32),
            jax.ShapeDtypeStruct(own.shape, bf16),
        ],
        in_specs=[smem] + [hbm] * 2,
        out_specs=[vmem] * 6,
        scratch_shapes=[pltpu.VMEM(code.shape, f32), pltpu.SemaphoreType.DMA((2,))],
        compiler_params=pltpu.CompilerParams(vmem_limit_bytes=16 * mib),
        cost_estimate=pl.CostEstimate(flops=100 * stations * lanes, bytes_accessed=16 * stations * lanes, transcendentals=0),
    )(place, own, code)

    early = max(1, steps // 3)
    cost = lambda part: pl.CostEstimate(
        flops=16 * part * stations * lanes, bytes_accessed=4 * part * stations * lanes, transcendentals=0
    )
    limit = pltpu.CompilerParams(vmem_limit_bytes=16 * mib)
    made = lambda part: jax.ShapeDtypeStruct((part, 2 * stations, lanes), bf16)
    held, reach, responses = own, (0,), []
    for cut, bit in enumerate(bits):
        came = lax.ppermute(held, "chan", [(j, j ^ bit) for j in range(count)])
        kept = jax.ShapeDtypeStruct(held.shape, bf16)
        if cut == 0:
            *base, phase_re, phase_im, held = make_tables()
        elif cut == 1:
            response, held, *spread = pl.pallas_call(
                lambda *refs: first_kernel(cells, taps, variants, width, *refs),
                out_shape=[made(early), kept] + [jax.ShapeDtypeStruct((steps, 8, lanes), f32)] * 2,
                in_specs=[smem] + [vmem] * 5,
                out_specs=[vmem] * 4,
                scratch_shapes=[pltpu.VMEM((variants * 128, lanes), bf16)] * 2,
                compiler_params=limit,
                cost_estimate=cost(early),
            )(place, held, shapes, *base)
            responses.append(response)
        elif cut == 2:
            response, held = pl.pallas_call(
                lambda *refs: second_kernel(early, variants, *refs),
                out_shape=[made(steps - early), kept],
                in_specs=[vmem] * 6,
                out_specs=[vmem] * 2,
                compiler_params=limit,
                cost_estimate=cost(steps - early),
            )(held, *base, *spread)
            responses.append(response)
        masks = [reach, tuple(m ^ bit for m in reach)]
        reach = sum(masks, ())
        blocks = [held, came]
        held = jnp.concatenate(blocks)

    x = (2.0 * np.arange(chans) + 1.0 - chans) / chans
    norm = [
        float(1.0 / np.sqrt(np.sum(x ** (2 * k))) / (times * stations * taps * taps) * (16.0 / chans) ** k)
        for k in range(3)
    ]
    groups = (len(blocks), len(responses))
    return pl.pallas_call(
        lambda *refs: image_kernel(chans, width, norm, masks, groups, *refs),
        out_shape=jax.ShapeDtypeStruct((3, height, width), f32),
        in_specs=[smem] + [vmem] * (2 + sum(groups)),
        out_specs=vmem,
        scratch_shapes=[
            pltpu.VMEM((2 * times, stations, chans), f32),
            pltpu.VMEM((planes, stations), f32),
            pltpu.VMEM((planes, stations), f32),
            pltpu.VMEM((2 * planes, 2 * stations), bf16),
            pltpu.VMEM((2 * planes, 2 * stations), bf16),
            pltpu.VMEM((3, steps, lanes + 128), f32),
            pltpu.VMEM((-(-width // 128), height, 128), f32),
        ],
        compiler_params=pltpu.CompilerParams(vmem_limit_bytes=32 * mib),
        cost_estimate=pl.CostEstimate(
            flops=8 * steps * planes * stations * lanes, bytes_accessed=4 * steps * stations * lanes, transcendentals=0
        ),
    )(place, phase_re, phase_im, *blocks, *responses)


def solution(mesh):
    cells = 768
    placed = (P(None, None, None, "chan"), P(), P(), P(), P())
    return jax.shard_map(
        lambda *args: local(cells, *args), mesh=mesh, in_specs=placed, out_specs=P(None, "chan", "row"), check_vma=False
    )
```

```python
import jax
import jax.numpy as jnp
import numpy as np
from jax import lax
from jax.experimental import pallas as pl
from jax.experimental.pallas import tpu as pltpu
from jax.sharding import PartitionSpec as P

TILE = 512
STEP = 8


def wave_fit(terms=6):
    nodes = 0.125 + 0.125 * np.cos(np.pi * (np.arange(200) + 0.5) / 200)
    root = np.sqrt(nodes)
    fit = np.polynomial.polynomial.polyfit
    cosine = fit(nodes, np.cos(2 * np.pi * root), terms - 1)
    sine = fit(nodes, np.sin(2 * np.pi * root) / root, terms - 1)
    return [float(c) for c in cosine], [float(c) for c in sine]


COS_FIT, SIN_FIT = wave_fit()


def horner(coefs, x):
    value = jnp.full_like(x, coefs[-1])
    for c in coefs[-2::-1]:
        value = value * x + c
    return value


def wave(product, cells):
    turns = product * (1.0 / cells)
    part = (product - cells * jnp.round(turns)) * (1.0 / cells)
    square = part * part
    return horner(COS_FIT, square), -part * horner(SIN_FIT, square)


def whole_of(shape, axis):
    return lax.broadcasted_iota(jnp.int32, shape, axis)


def split(value):
    high = value.astype(jnp.bfloat16)
    return high, (value - high.astype(jnp.float32)).astype(jnp.bfloat16)


def station_column(values, stations):
    return jnp.broadcast_to(values, (128, stations)).T


def table_kernel(
    cells, width, place, held_in, joined_in, table_in,
    base_re, base_im, pick, spread_re, spread_im, phase_re, phase_im, held, joined, table, arrived
):
    copies = [
        pltpu.make_async_copy(source, target, arrived.at[n])
        for n, (source, target) in enumerate((
            (joined_in, joined), (table_in, table), (held_in, held),
        ))
    ]
    for copy in copies:
        copy.start()
    for copy in copies:
        copy.wait()
    stations = joined.shape[1]
    steps, lanes = spread_re.shape[0], spread_re.shape[2]
    taps = table.shape[1]
    variants = table.shape[0] // taps
    first_row = place[1].astype(jnp.float32)
    first_col = place[2].astype(jnp.float32)
    code = joined[...].astype(jnp.float32)
    rows = jnp.floor((code + 0.5) * (1.0 / (cells * variants)))
    code = code - rows * float(cells * variants)
    cols = jnp.floor((code + 0.5) * (1.0 / variants))
    pick[...] = station_column(code - cols * float(variants), stations).astype(jnp.int32)
    row_of = station_column(rows, stations)
    col_of = station_column(cols, stations)
    start = first_row + float(STEP) * whole_of((steps, stations), 0).astype(jnp.float32)
    phase_re[...], phase_im[...] = wave(start * rows, cells)

    def down_across(shape, start):
        lane = whole_of(shape, 1) + start
        down = jnp.zeros(shape, jnp.float32)
        for p in range(1, STEP):
            down = jnp.where(lane >= p * width, float(p), down)
        return down, lane.astype(jnp.float32) - down * width + first_col

    pace = lanes // STEP * 2
    leaps = [wave(row_of * float(p), cells) for p in (2, 4)]
    for tile in range(pace // 128):
        down, across = down_across((stations, 128), tile * 128)
        near = [wave(row_of * down + col_of * across, cells)]
        for leap_re, leap_im in leaps:
            near += [(re * leap_re - im * leap_im, re * leap_im + im * leap_re) for re, im in near]
        for p, (real, imag) in enumerate(near):
            at = slice(p * pace + tile * 128, p * pace + (tile + 1) * 128)
            base_re[:, at], base_im[:, at] = real, imag

    down, across = down_across((taps, lanes), 0)
    tap = whole_of((taps, lanes), 0).astype(jnp.float32)
    kernels = table[...]

    def over_columns(value):
        high, low = split(value)
        return jnp.dot(kernels, high, preferred_element_type=jnp.float32) + jnp.dot(
            kernels, low, preferred_element_type=jnp.float32
        )

    half_re, half_im = [over_columns(value) for value in wave(tap * across, cells)]
    turn_re, turn_im = wave(tap * down, cells)
    tall = -(-steps // 16) * 16
    lane = whole_of((tall, 6 * taps), 1)
    start = first_row + float(STEP) * whole_of((tall, 6 * taps), 0).astype(jnp.float32)
    left_re, left_im = wave(start * (lane % taps).astype(jnp.float32), cells)
    value = jnp.where(lane // taps % 2 == 0, left_re, -left_im)
    high, low = split(value)
    left = jnp.where(lane // (2 * taps) == 1, low.astype(jnp.float32), high.astype(jnp.float32)).astype(jnp.bfloat16)
    for o in range(variants):
        rows_o = slice(o * taps, (o + 1) * taps)
        real = turn_re * half_re[rows_o] - turn_im * half_im[rows_o]
        imag = turn_re * half_im[rows_o] + turn_im * half_re[rows_o]
        for target, one, two in ((spread_re, real, imag), (spread_im, imag, -real)):
            one_high, one_low = split(one)
            two_high, two_low = split(two)
            right = jnp.concatenate([one_high, two_high, one_high, two_high, one_low, two_low], axis=0)
            target[:, o, :] = jnp.dot(left, right, preferred_element_type=jnp.float32)[:steps]


def response_kernel(first, held, base_re, base_im, pick, spread_re, spread_im, response, kept):
    kept[...] = held[...]
    parts, stations, lanes = response.shape[0], base_re.shape[0], base_re.shape[1]
    joint = 2 if parts % 2 == 0 else 1

    def some(i, carry):
        for tile in range(lanes // 128):
            at = slice(tile * 128, (tile + 1) * 128)
            tables = [
                (spread_re[first + joint * i + j, :, at], spread_im[first + joint * i + j, :, at]) for j in range(joint)
            ]
            for group in range(stations // 16):
                made = [([], []) for j in range(joint)]
                for half in range(2):
                    sub = slice(group * 16 + half * 8, group * 16 + half * 8 + 8)
                    index = pick[sub, :]
                    br = base_re[sub, at]
                    bi = base_im[sub, at]
                    for j in range(joint):
                        sr = jnp.take_along_axis(tables[j][0], index, axis=0)
                        si = jnp.take_along_axis(tables[j][1], index, axis=0)
                        made[j][0].append(br * sr - bi * si)
                        made[j][1].append(br * si + bi * sr)
                pair = slice(group * 16, group * 16 + 16)
                low = slice(stations + group * 16, stations + group * 16 + 16)
                for j in range(joint):
                    response[joint * i + j, pair, at] = jnp.concatenate(made[j][0], axis=0).astype(jnp.bfloat16)
                    response[joint * i + j, low, at] = jnp.concatenate(made[j][1], axis=0).astype(jnp.bfloat16)
        return carry

    lax.fori_loop(0, parts // joint, some, 0)


def image_kernel(
    chans, width, norm, masks, groups, place, phase_re, phase_im, *refs
):
    blocks, responses = refs[:groups[0]], refs[groups[0]:sum(groups)]
    out, turned, volt_re, volt_im, x_a, x_b, sums, strips = refs[sum(groups):]
    planes, stations = volt_re.shape
    steps, lanes = phase_re.shape[0], responses[0].shape[2]
    sheets = turned.shape[0]
    each = stations // len(sum(masks, ()))

    for block, held in zip(blocks, masks):
        value = block[...].astype(jnp.float32)
        for n, mask in enumerate(held):
            at = pl.multiple_of((place[0] ^ mask) * each, 8)
            for sheet in range(sheets):
                line = (n * sheets + sheet) * each
                turned[sheet, pl.ds(at, each), :] = value[line:line + each]
    times = sheets // 2
    for sheet in range(sheets):
        target = volt_re if sheet < times else volt_im
        facing = turned[sheet].astype(jnp.bfloat16).T.astype(jnp.float32)
        for g in range(chans // 8):
            at = (g * times + sheet % times) * 8
            target[at:at + 8, :] = facing[g * 8:g * 8 + 8]
    span = 8 * times

    def prepare(q, x_out):
        pr = phase_re[pl.ds(q, 1), :]
        pi = phase_im[pl.ds(q, 1), :]
        for g in range(chans // 8):
            vr = volt_re[g * span:(g + 1) * span, :]
            vi = volt_im[g * span:(g + 1) * span, :]
            xr = (vr * pr - vi * pi).astype(jnp.bfloat16)
            xi = (vr * pi + vi * pr).astype(jnp.bfloat16)
            real = slice(2 * g * span, (2 * g + 1) * span)
            imag = slice((2 * g + 1) * span, (2 * g + 2) * span)
            x_out[real, :stations] = xr
            x_out[real, stations:] = -xi
            x_out[imag, :stations] = xi
            x_out[imag, stations:] = xr

    top = chans // 8
    step_of = top + (2.0 * whole_of((8, TILE), 0).astype(jnp.float32) + 1.0 - chans) * 0.0625

    def collect(q, tile, field):
        s0, s1, s2 = None, None, None
        for g in range(top):
            for t in range(2 * times):
                line = (g * 2 * times + t) * 8
                part = field[line:line + 8, :]
                total = part * part if t == 0 else total + part * part
            s0 = total if g == 0 else s0 + total
            s1 = s0 if g == 0 else s1 + s0
            s2 = s1 if g == 0 else s2 + s1
        first = step_of * s0 - s1
        second = step_of * (step_of * s0 - 2.0 * s1) + (2.0 * s2 - s1)
        for k, value in enumerate((s0, first, second)):
            sums[k, pl.ds(q, 1), tile * TILE:(tile + 1) * TILE] = norm[k] * jnp.sum(value, axis=0, keepdims=True)

    tiles = lanes // TILE
    xs = (x_a, x_b)
    prepare(0, x_a)

    def chunk(q, turn, response, index):
        for n in range(tiles):
            field = jnp.dot(
                xs[turn][...], response[index, :, n * TILE:(n + 1) * TILE], preferred_element_type=jnp.float32
            )
            if n == 0:
                prepare(jnp.minimum(q + 1, steps - 1), xs[1 - turn])
            collect(q, n, field)

    base, turn = 0, 0
    for response in responses:
        here = response.shape[0]

        def two(i, carry):
            for j in range(2):
                chunk(base + 2 * i + j, (turn + j) % 2, response, 2 * i + j)
            return carry

        lax.fori_loop(0, here // 2, two, 0)
        if here % 2:
            chunk(base + here - 1, turn, response, here - 1)
        base, turn = base + here, (turn + here) % 2
    for k in range(3):
        for p in range(STEP):
            for j in range(strips.shape[0]):
                at = p * width + j * 128
                strips[j, pl.ds(p, steps, stride=STEP), :] = sums[k, :, at:at + 128]
        for j in range(strips.shape[0]):
            left = min(128, width - j * 128)
            out[k, :, j * 128:j * 128 + left] = strips[j, :, :left]


def local(cells, voltages, kernel_table, station_rows, station_cols, kernel_offset):
    times, chans = voltages.shape[1], voltages.shape[2]
    stations = station_rows.shape[0]
    variants, taps = kernel_table.shape[0], kernel_table.shape[1]
    count = lax.axis_size("chan")
    height = cells // count
    width = cells // lax.axis_size("row")
    here = lax.axis_index("chan")
    steps = height // STEP
    lanes = STEP * width
    planes = times * chans
    place = jnp.stack([here, here * height, lax.axis_index("row") * width]).astype(jnp.int32)
    vmem = pl.BlockSpec(memory_space=pltpu.VMEM)
    smem = pl.BlockSpec(memory_space=pltpu.SMEM)
    f32, bf16 = jnp.float32, jnp.bfloat16
    mib = 1024 * 1024

    bits = []
    while (1 << len(bits)) < count:
        bits.append(count >> (len(bits) + 1))
    hbm = pl.BlockSpec(memory_space=pltpu.HBM)
    joined = ((station_rows * cells + station_cols) * variants + kernel_offset).reshape(1, stations)
    own = voltages.transpose(0, 1, 3, 2).reshape(2 * times * voltages.shape[3], chans)
    make_tables = lambda: pl.pallas_call(
        lambda *refs: table_kernel(cells, width, *refs),
        out_shape=[
            jax.ShapeDtypeStruct((stations, lanes), f32),
            jax.ShapeDtypeStruct((stations, lanes), f32),
            jax.ShapeDtypeStruct((stations, 128), jnp.int32),
            jax.ShapeDtypeStruct((steps, 8, lanes), f32),
            jax.ShapeDtypeStruct((steps, 8, lanes), f32),
            jax.ShapeDtypeStruct((steps, stations), f32),
            jax.ShapeDtypeStruct((steps, stations), f32),
            jax.ShapeDtypeStruct(own.shape, bf16),
        ],
        in_specs=[smem] + [hbm] * 3,
        out_specs=[vmem] * 8,
        scratch_shapes=[
            pltpu.VMEM((1, stations), jnp.int32),
            pltpu.VMEM((variants * taps, taps), bf16),
            pltpu.SemaphoreType.DMA((3,)),
        ],
        compiler_params=pltpu.CompilerParams(vmem_limit_bytes=16 * mib),
        cost_estimate=pl.CostEstimate(flops=100 * stations * lanes, bytes_accessed=16 * stations * lanes, transcendentals=0),
    )(place, own, joined, kernel_table.reshape(variants * taps, taps))

    ahead = steps // 2
    shares = [(0, steps - ahead), (steps - ahead, ahead)]
    held, reach, responses = own, (0,), []
    for cut, bit in enumerate(bits):
        came = lax.ppermute(held, "chan", [(j, j ^ bit) for j in range(count)])
        if cut == 0:
            *tables, phase_re, phase_im, held = make_tables()
        elif cut <= len(shares):
            first, part = shares[cut - 1]
            response, held = pl.pallas_call(
                lambda *refs, first=first: response_kernel(first, *refs),
                out_shape=[
                    jax.ShapeDtypeStruct((part, 2 * stations, lanes), bf16),
                    jax.ShapeDtypeStruct(held.shape, bf16),
                ],
                in_specs=[vmem] * 6,
                out_specs=[vmem] * 2,
                compiler_params=pltpu.CompilerParams(vmem_limit_bytes=16 * mib),
                cost_estimate=pl.CostEstimate(
                    flops=16 * part * stations * lanes, bytes_accessed=4 * part * stations * lanes, transcendentals=0
                ),
            )(held, *tables)
            responses.append(response)
        masks = [reach, tuple(m ^ bit for m in reach)]
        reach = sum(masks, ())
        blocks = [held, came]
        held = jnp.concatenate(blocks)

    x = (2.0 * np.arange(chans) + 1.0 - chans) / chans
    norm = [
        float(1.0 / np.sqrt(np.sum(x ** (2 * k))) / (times * stations * taps * taps) * (16.0 / chans) ** k)
        for k in range(3)
    ]
    groups = (len(blocks), len(responses))
    return pl.pallas_call(
        lambda *refs: image_kernel(chans, width, norm, masks, groups, *refs),
        out_shape=jax.ShapeDtypeStruct((3, height, width), f32),
        in_specs=[smem] + [vmem] * (2 + sum(groups)),
        out_specs=vmem,
        scratch_shapes=[
            pltpu.VMEM((2 * times, stations, chans), f32),
            pltpu.VMEM((planes, stations), f32),
            pltpu.VMEM((planes, stations), f32),
            pltpu.VMEM((2 * planes, 2 * stations), bf16),
            pltpu.VMEM((2 * planes, 2 * stations), bf16),
            pltpu.VMEM((3, steps, lanes + 128), f32),
            pltpu.VMEM((-(-width // 128), height, 128), f32),
        ],
        compiler_params=pltpu.CompilerParams(vmem_limit_bytes=32 * mib),
        cost_estimate=pl.CostEstimate(
            flops=8 * steps * planes * stations * lanes, bytes_accessed=4 * steps * stations * lanes, transcendentals=0
        ),
    )(place, phase_re, phase_im, *blocks, *responses)


def solution(mesh):
    cells = 768
    placed = (P(None, None, None, "chan"), P(), P(), P(), P())
    return jax.shard_map(
        lambda *args: local(cells, *args), mesh=mesh, in_specs=placed, out_specs=P(None, "chan", "row"), check_vma=False
    )
```

```python
import jax
import jax.numpy as jnp
import numpy as np
from jax import lax
from jax.experimental import pallas as pl
from jax.experimental.pallas import tpu as pltpu
from jax.sharding import PartitionSpec as P

TILE = 512
STEP = 8


def wave_fit(terms=6):
    nodes = 0.125 + 0.125 * np.cos(np.pi * (np.arange(200) + 0.5) / 200)
    root = np.sqrt(nodes)
    fit = np.polynomial.polynomial.polyfit
    cosine = fit(nodes, np.cos(2 * np.pi * root), terms - 1)
    sine = fit(nodes, np.sin(2 * np.pi * root) / root, terms - 1)
    return [float(c) for c in cosine], [float(c) for c in sine]


COS_FIT, SIN_FIT = wave_fit()


def horner(coefs, x):
    value = jnp.full_like(x, coefs[-1])
    for c in coefs[-2::-1]:
        value = value * x + c
    return value


def wave(product, cells):
    turns = product * (1.0 / cells)
    part = (product - cells * jnp.round(turns)) * (1.0 / cells)
    square = part * part
    return horner(COS_FIT, square), -part * horner(SIN_FIT, square)


def whole_of(shape, axis):
    return lax.broadcasted_iota(jnp.int32, shape, axis)


def split(value):
    high = value.astype(jnp.bfloat16)
    return high, (value - high.astype(jnp.float32)).astype(jnp.bfloat16)


def station_column(values, stations):
    return jnp.broadcast_to(values, (128, stations)).T


def table_kernel(
    cells, width, place, held_in, joined_in, table_in,
    base_re, base_im, pick, spread_re, spread_im, phase_re, phase_im, held, joined, table, arrived
):
    copies = [
        pltpu.make_async_copy(source, target, arrived.at[n])
        for n, (source, target) in enumerate((
            (joined_in, joined), (table_in, table), (held_in, held),
        ))
    ]
    for copy in copies:
        copy.start()
    for copy in copies:
        copy.wait()
    stations = joined.shape[1]
    steps, lanes = spread_re.shape[0], spread_re.shape[2]
    taps = table.shape[1]
    variants = table.shape[0] // taps
    first_row = place[1].astype(jnp.float32)
    first_col = place[2].astype(jnp.float32)
    code = joined[...].astype(jnp.float32)
    rows = jnp.floor((code + 0.5) * (1.0 / (cells * variants)))
    code = code - rows * float(cells * variants)
    cols = jnp.floor((code + 0.5) * (1.0 / variants))
    pick[...] = station_column(code - cols * float(variants), stations).astype(jnp.int32)
    row_of = station_column(rows, stations)
    col_of = station_column(cols, stations)
    start = first_row + float(STEP) * whole_of((steps, stations), 0).astype(jnp.float32)
    phase_re[...], phase_im[...] = wave(start * rows, cells)

    def down_across(shape, start):
        lane = whole_of(shape, 1) + start
        down = jnp.zeros(shape, jnp.float32)
        for p in range(1, STEP):
            down = jnp.where(lane >= p * width, float(p), down)
        return down, lane.astype(jnp.float32) - down * width + first_col

    pace = lanes // STEP * 2
    leaps = [wave(row_of * float(p), cells) for p in (2, 4)]
    for tile in range(pace // 128):
        down, across = down_across((stations, 128), tile * 128)
        near = [wave(row_of * down + col_of * across, cells)]
        for leap_re, leap_im in leaps:
            near += [(re * leap_re - im * leap_im, re * leap_im + im * leap_re) for re, im in near]
        for p, (real, imag) in enumerate(near):
            at = slice(p * pace + tile * 128, p * pace + (tile + 1) * 128)
            base_re[:, at], base_im[:, at] = real, imag

    down, across = down_across((taps, lanes), 0)
    tap = whole_of((taps, lanes), 0).astype(jnp.float32)
    kernels = table[...]

    def over_columns(value):
        high, low = split(value)
        return jnp.dot(kernels, high, preferred_element_type=jnp.float32) + jnp.dot(
            kernels, low, preferred_element_type=jnp.float32
        )

    half_re, half_im = [over_columns(value) for value in wave(tap * across, cells)]
    turn_re, turn_im = wave(tap * down, cells)
    tall = -(-steps // 16) * 16
    lane = whole_of((tall, 6 * taps), 1)
    start = first_row + float(STEP) * whole_of((tall, 6 * taps), 0).astype(jnp.float32)
    left_re, left_im = wave(start * (lane % taps).astype(jnp.float32), cells)
    value = jnp.where(lane // taps % 2 == 0, left_re, -left_im)
    high, low = split(value)
    left = jnp.where(lane // (2 * taps) == 1, low.astype(jnp.float32), high.astype(jnp.float32)).astype(jnp.bfloat16)
    for o in range(variants):
        rows_o = slice(o * taps, (o + 1) * taps)
        real = turn_re * half_re[rows_o] - turn_im * half_im[rows_o]
        imag = turn_re * half_im[rows_o] + turn_im * half_re[rows_o]
        for target, one, two in ((spread_re, real, imag), (spread_im, imag, -real)):
            one_high, one_low = split(one)
            two_high, two_low = split(two)
            right = jnp.concatenate([one_high, two_high, one_high, two_high, one_low, two_low], axis=0)
            target[:, o, :] = jnp.dot(left, right, preferred_element_type=jnp.float32)[:steps]


def response_kernel(first, held, base_re, base_im, pick, spread_re, spread_im, response, kept):
    kept[...] = held[...]
    parts, stations, lanes = response.shape[0], base_re.shape[0], base_re.shape[1]
    joint = next(n for n in (3, 2, 1) if parts % n == 0)

    def some(i, carry):
        for tile in range(lanes // 128):
            at = slice(tile * 128, (tile + 1) * 128)
            tables = [
                (spread_re[first + joint * i + j, :, at], spread_im[first + joint * i + j, :, at]) for j in range(joint)
            ]
            for group in range(stations // 16):
                made = [([], []) for j in range(joint)]
                for half in range(2):
                    sub = slice(group * 16 + half * 8, group * 16 + half * 8 + 8)
                    index = pick[sub, :]
                    br = base_re[sub, at]
                    bi = base_im[sub, at]
                    for j in range(joint):
                        sr = jnp.take_along_axis(tables[j][0], index, axis=0)
                        si = jnp.take_along_axis(tables[j][1], index, axis=0)
                        made[j][0].append(br * sr - bi * si)
                        made[j][1].append(br * si + bi * sr)
                pair = slice(group * 16, group * 16 + 16)
                low = slice(stations + group * 16, stations + group * 16 + 16)
                for j in range(joint):
                    response[joint * i + j, pair, at] = jnp.concatenate(made[j][0], axis=0).astype(jnp.bfloat16)
                    response[joint * i + j, low, at] = jnp.concatenate(made[j][1], axis=0).astype(jnp.bfloat16)
        return carry

    lax.fori_loop(0, parts // joint, some, 0)


def image_kernel(
    chans, width, norm, masks, groups, place, phase_re, phase_im, *refs
):
    blocks, responses = refs[:groups[0]], refs[groups[0]:sum(groups)]
    out, turned, volt_re, volt_im, x_a, x_b, sums, strips = refs[sum(groups):]
    planes, stations = volt_re.shape
    steps, lanes = phase_re.shape[0], responses[0].shape[2]
    sheets = turned.shape[0]
    each = stations // len(sum(masks, ()))

    for block, held in zip(blocks, masks):
        value = block[...].astype(jnp.float32)
        for n, mask in enumerate(held):
            at = pl.multiple_of((place[0] ^ mask) * each, 8)
            for sheet in range(sheets):
                line = (n * sheets + sheet) * each
                turned[sheet, pl.ds(at, each), :] = value[line:line + each]
    times = sheets // 2
    for sheet in range(sheets):
        target = volt_re if sheet < times else volt_im
        facing = turned[sheet].astype(jnp.bfloat16).T.astype(jnp.float32)
        for g in range(chans // 8):
            at = (g * times + sheet % times) * 8
            target[at:at + 8, :] = facing[g * 8:g * 8 + 8]
    span = 8 * times

    def prepare(q, x_out):
        pr = phase_re[pl.ds(q, 1), :]
        pi = phase_im[pl.ds(q, 1), :]
        for g in range(chans // 8):
            vr = volt_re[g * span:(g + 1) * span, :]
            vi = volt_im[g * span:(g + 1) * span, :]
            xr = (vr * pr - vi * pi).astype(jnp.bfloat16)
            xi = (vr * pi + vi * pr).astype(jnp.bfloat16)
            real = slice(2 * g * span, (2 * g + 1) * span)
            imag = slice((2 * g + 1) * span, (2 * g + 2) * span)
            x_out[real, :stations] = xr
            x_out[real, stations:] = -xi
            x_out[imag, :stations] = xi
            x_out[imag, stations:] = xr

    top = chans // 8
    step_of = top + (2.0 * whole_of((8, TILE), 0).astype(jnp.float32) + 1.0 - chans) * 0.0625

    def collect(q, tile, field):
        s0, s1, s2 = None, None, None
        for g in range(top):
            for t in range(2 * times):
                line = (g * 2 * times + t) * 8
                part = field[line:line + 8, :]
                total = part * part if t == 0 else total + part * part
            s0 = total if g == 0 else s0 + total
            s1 = s0 if g == 0 else s1 + s0
            s2 = s1 if g == 0 else s2 + s1
        first = step_of * s0 - s1
        second = step_of * (step_of * s0 - 2.0 * s1) + (2.0 * s2 - s1)
        for k, value in enumerate((s0, first, second)):
            sums[k, pl.ds(q, 1), tile * TILE:(tile + 1) * TILE] = norm[k] * jnp.sum(value, axis=0, keepdims=True)

    tiles = lanes // TILE
    xs = (x_a, x_b)
    prepare(0, x_a)

    def chunk(q, turn, response, index):
        for n in range(tiles):
            field = jnp.dot(
                xs[turn][...], response[index, :, n * TILE:(n + 1) * TILE], preferred_element_type=jnp.float32
            )
            if n == 0:
                prepare(jnp.minimum(q + 1, steps - 1), xs[1 - turn])
            collect(q, n, field)

    base, turn = 0, 0
    for response in responses:
        here = response.shape[0]

        def two(i, carry):
            for j in range(2):
                chunk(base + 2 * i + j, (turn + j) % 2, response, 2 * i + j)
            return carry

        lax.fori_loop(0, here // 2, two, 0)
        if here % 2:
            chunk(base + here - 1, turn, response, here - 1)
        base, turn = base + here, (turn + here) % 2
    for k in range(3):
        for p in range(STEP):
            for j in range(strips.shape[0]):
                at = p * width + j * 128
                strips[j, pl.ds(p, steps, stride=STEP), :] = sums[k, :, at:at + 128]
        for j in range(strips.shape[0]):
            left = min(128, width - j * 128)
            out[k, :, j * 128:j * 128 + left] = strips[j, :, :left]


def local(cells, voltages, kernel_table, station_rows, station_cols, kernel_offset):
    times, chans = voltages.shape[1], voltages.shape[2]
    stations = station_rows.shape[0]
    variants, taps = kernel_table.shape[0], kernel_table.shape[1]
    count = lax.axis_size("chan")
    height = cells // count
    width = cells // lax.axis_size("row")
    here = lax.axis_index("chan")
    steps = height // STEP
    lanes = STEP * width
    planes = times * chans
    place = jnp.stack([here, here * height, lax.axis_index("row") * width]).astype(jnp.int32)
    vmem = pl.BlockSpec(memory_space=pltpu.VMEM)
    smem = pl.BlockSpec(memory_space=pltpu.SMEM)
    f32, bf16 = jnp.float32, jnp.bfloat16
    mib = 1024 * 1024

    bits = []
    while (1 << len(bits)) < count:
        bits.append(count >> (len(bits) + 1))
    hbm = pl.BlockSpec(memory_space=pltpu.HBM)
    joined = ((station_rows * cells + station_cols) * variants + kernel_offset).reshape(1, stations)
    own = voltages.transpose(0, 1, 3, 2).reshape(2 * times * voltages.shape[3], chans)
    make_tables = lambda: pl.pallas_call(
        lambda *refs: table_kernel(cells, width, *refs),
        out_shape=[
            jax.ShapeDtypeStruct((stations, lanes), f32),
            jax.ShapeDtypeStruct((stations, lanes), f32),
            jax.ShapeDtypeStruct((stations, 128), jnp.int32),
            jax.ShapeDtypeStruct((steps, 8, lanes), f32),
            jax.ShapeDtypeStruct((steps, 8, lanes), f32),
            jax.ShapeDtypeStruct((steps, stations), f32),
            jax.ShapeDtypeStruct((steps, stations), f32),
            jax.ShapeDtypeStruct(own.shape, bf16),
        ],
        in_specs=[smem] + [hbm] * 3,
        out_specs=[vmem] * 8,
        scratch_shapes=[
            pltpu.VMEM((1, stations), jnp.int32),
            pltpu.VMEM((variants * taps, taps), bf16),
            pltpu.SemaphoreType.DMA((3,)),
        ],
        compiler_params=pltpu.CompilerParams(vmem_limit_bytes=16 * mib),
        cost_estimate=pl.CostEstimate(flops=100 * stations * lanes, bytes_accessed=16 * stations * lanes, transcendentals=0),
    )(place, own, joined, kernel_table.reshape(variants * taps, taps))

    ahead = steps // 2
    shares = [(0, steps - ahead), (steps - ahead, ahead)]
    held, reach, responses = own, (0,), []
    for cut, bit in enumerate(bits):
        came = lax.ppermute(held, "chan", [(j, j ^ bit) for j in range(count)])
        if cut == 0:
            *tables, phase_re, phase_im, held = make_tables()
        elif cut <= len(shares):
            first, part = shares[cut - 1]
            response, held = pl.pallas_call(
                lambda *refs, first=first: response_kernel(first, *refs),
                out_shape=[
                    jax.ShapeDtypeStruct((part, 2 * stations, lanes), bf16),
                    jax.ShapeDtypeStruct(held.shape, bf16),
                ],
                in_specs=[vmem] * 6,
                out_specs=[vmem] * 2,
                compiler_params=pltpu.CompilerParams(vmem_limit_bytes=16 * mib),
                cost_estimate=pl.CostEstimate(
                    flops=16 * part * stations * lanes, bytes_accessed=4 * part * stations * lanes, transcendentals=0
                ),
            )(held, *tables)
            responses.append(response)
        masks = [reach, tuple(m ^ bit for m in reach)]
        reach = sum(masks, ())
        blocks = [held, came]
        held = jnp.concatenate(blocks)

    x = (2.0 * np.arange(chans) + 1.0 - chans) / chans
    norm = [
        float(1.0 / np.sqrt(np.sum(x ** (2 * k))) / (times * stations * taps * taps) * (16.0 / chans) ** k)
        for k in range(3)
    ]
    groups = (len(blocks), len(responses))
    return pl.pallas_call(
        lambda *refs: image_kernel(chans, width, norm, masks, groups, *refs),
        out_shape=jax.ShapeDtypeStruct((3, height, width), f32),
        in_specs=[smem] + [vmem] * (2 + sum(groups)),
        out_specs=vmem,
        scratch_shapes=[
            pltpu.VMEM((2 * times, stations, chans), f32),
            pltpu.VMEM((planes, stations), f32),
            pltpu.VMEM((planes, stations), f32),
            pltpu.VMEM((2 * planes, 2 * stations), bf16),
            pltpu.VMEM((2 * planes, 2 * stations), bf16),
            pltpu.VMEM((3, steps, lanes + 128), f32),
            pltpu.VMEM((-(-width // 128), height, 128), f32),
        ],
        compiler_params=pltpu.CompilerParams(vmem_limit_bytes=32 * mib),
        cost_estimate=pl.CostEstimate(
            flops=8 * steps * planes * stations * lanes, bytes_accessed=4 * steps * stations * lanes, transcendentals=0
        ),
    )(place, phase_re, phase_im, *blocks, *responses)


def solution(mesh):
    cells = 768
    placed = (P(None, None, None, "chan"), P(), P(), P(), P())
    return jax.shard_map(
        lambda *args: local(cells, *args), mesh=mesh, in_specs=placed, out_specs=P(None, "chan", "row"), check_vma=False
    )
```
